128 devices in a mesh: section: 4 (over x), tensor: 8 (over z_lo, y), dp: 4 (over z_hi, core).
Axes of the slice: x: 4, y: 4, z: 4 (z_hi: 2, z_lo: 2; z = z_hi * 2 + z_lo), core: 2. Of those that a mesh axis runs over, the one named last changes fastest.
Arguments:
- cotangent: bfloat16 [512, 8192], P(None, 'dp'), may hold values from -6 to 6
- queries: bfloat16 [4, 512, 4096], P('section', 'dp', 'tensor'), may hold values from -120 to 120
- keys_values: bfloat16 [4, 1024, 2, 4096], P('section', 'dp', None, 'tensor'), may hold values from -4.5 to 4.5
- streams_in: bfloat16 [4, 512, 8192], P('section', None, 'dp'), may hold values from -6 to 6
- neighbours: bfloat16 [1024, 8192], P(None, 'dp'), may hold values from -6 to 6
- w_query: bfloat16 [4, 8192, 4096], P('section', 'dp', 'tensor'), may hold values from -0.25 to 0.25
- w_key_value: bfloat16 [4, 8192, 2, 4096], P('section', 'dp', None, 'tensor'), may hold values from -0.0625 to 0.0625
- w_out: bfloat16 [4, 4096, 8192], P('section', 'tensor', 'dp'), may hold values from -0.09375 to 0.09375
Outputs:
- d_streams: bfloat16 [4, 512, 8192], P('section', 'tensor', 'dp')
- d_neighbours: bfloat16 [1024, 8192], P(('section', 'tensor'), 'dp')
- grad_query: bfloat16 [4, 8192, 4096], P('section', 'dp', 'tensor')
- grad_key_value: bfloat16 [4, 8192, 2, 4096], P('section', 'dp', None, 'tensor')
- grad_out: bfloat16 [4, 4096, 8192], P('section', 'tensor', 'dp')
The draws below stay inside these ranges and needn't reach their ends.
All inputs are finite; a program needn't handle non-finite values.
Results may differ from the reference program's by a relative error of at most 0.035.
Values may be sent and summed in bfloat16 or wider, within the bound.
A program may use at most 128 MiB of HBM per device.

```python
import jax
import jax.numpy as jnp
from jax import lax

D = 8192
HEADS = 32
HDIM = 128
SPAN = 64
NTOK = 128
HID = 4096
TOKENS = 512
MROWS = 1024
N_SECTION = 4
N_TENSOR = 8


def shared_keys(key):
    base = jax.random.normal(key, (N_SECTION, MROWS, HID), jnp.float32)
    return jnp.clip(base, -4.0, 4.0)


def draw_keys_values(key, part):
    drawn_keys = shared_keys(key)
    key = jax.random.fold_in(key, 3)
    values = jnp.clip(jax.random.normal(jax.random.fold_in(key, 1), (N_SECTION, MROWS, HID), jnp.float32), -4.0, 4.0)
    return jnp.stack([drawn_keys, values], axis=2).astype(jnp.bfloat16)


def draw_queries(key, part):
    key = jax.random.fold_in(key, 5)
    result = jnp.clip(jax.random.normal(key, (N_SECTION, TOKENS, HID), jnp.float32), -4.0, 4.0)
    return result.astype(jnp.bfloat16)


def shard_levels(own_key, shape, cuts, low, largest):
    def one(axis_at, shards_of):
        heights = jax.random.uniform(jax.random.fold_in(jax.random.fold_in(own_key, 6), axis_at), (shards_of,), jnp.float32, low / len(cuts), largest / len(cuts))
        return jnp.repeat(jnp.exp(heights), shape[axis_at] // shards_of).reshape((-1,) + (1,) * (len(shape) - axis_at - 1))

    factor_of = one(*cuts[0])
    for cut in cuts[1:]:
        factor_of = factor_of * one(*cut)
    return factor_of


def normal_values(own_key, dims, spread, most, shards=(), held_as=jnp.bfloat16):
    array = spread * jax.random.normal(own_key, dims, jnp.float32)
    if shards:
        array = array * shard_levels(own_key, dims, shards, -0.22, 0.18)
    return jnp.clip(array, -most, most).astype(held_as)


def setup_inputs(seed: int = 0) -> dict:
    key_list = jax.random.split(jax.random.key(seed), 9)
    cotangent = normal_values(key_list[0], (TOKENS, D), 1.0, 6.0, ((1, 4),))
    queries = draw_queries(jax.random.fold_in(key_list[8], 71), 0)
    keys_values = draw_keys_values(jax.random.fold_in(key_list[8], 71), 0)
    streams_in = normal_values(key_list[3], (N_SECTION, TOKENS, D), 1.0, 6.0, ((0, 4), (2, 4)))
    neighbours = normal_values(key_list[4], (MROWS, D), 1.0, 6.0, ((1, 4),))
    w_query = normal_values(key_list[5], (N_SECTION, D, HID), (D // 16) ** -0.5, 0.25, ((0, 4), (1, 4), (2, 8)))
    w_key_value = normal_values(key_list[6], (N_SECTION, D, 2, HID), D ** -0.5, 0.0625, ((0, 4), (1, 4), (3, 8)))
    w_out = normal_values(key_list[7], (N_SECTION, HID, D), HID ** -0.5, 0.09375, ((0, 4), (1, 8), (2, 4)))
    return {"cotangent": cotangent, "queries": queries, "keys_values": keys_values, "streams_in": streams_in, "neighbours": neighbours, "w_query": w_query, "w_key_value": w_key_value, "w_out": w_out}


def softmax_parts(query_rows, pair_rows):
    spans = query_rows.shape[0] // SPAN
    query_heads = query_rows.astype(jnp.float32).reshape(spans, SPAN, HEADS, HDIM)
    key_heads = pair_rows[:, 0].astype(jnp.float32).reshape(spans, NTOK, HEADS, HDIM)
    value_heads = pair_rows[:, 1].astype(jnp.float32).reshape(spans, NTOK, HEADS, HDIM)
    inv_scale = HDIM ** -0.5
    scores = jnp.einsum('cqhd,ckhd->chqk', query_heads, key_heads) * inv_scale
    row_max = jnp.max(scores, axis=-1, keepdims=True)
    expo = jnp.exp(scores - row_max)
    prob_full = expo / jnp.sum(expo, axis=-1, keepdims=True)
    prob_half = prob_full.astype(jnp.bfloat16)
    attended = jnp.einsum('chqk,ckhd->cqhd', prob_half.astype(jnp.float32), value_heads)
    attended = attended.astype(jnp.bfloat16).reshape(query_rows.shape)
    return query_heads, key_heads, value_heads, prob_full, prob_half, attended


def reference(cotangent, queries, keys_values, streams_in, neighbours, w_query, w_key_value, w_out):
    grad_in = cotangent
    stream_list = [None] * N_SECTION
    query_list = [None] * N_SECTION
    pair_list = [None] * N_SECTION
    outer_list = [None] * N_SECTION
    neighbour_total = jnp.zeros((MROWS, D), jnp.float32)
    group_width = HID // N_TENSOR
    inv_scale = HDIM ** -0.5
    for section_index in reversed(range(N_SECTION)):
        query_rows = queries[section_index]
        pair_rows = keys_values[section_index]
        query_heads, key_heads, value_heads, prob_full, prob_half, attended = softmax_parts(query_rows, pair_rows)
        spans = query_rows.shape[0] // SPAN
        grad_att = jnp.dot(grad_in, w_out[section_index].T, preferred_element_type=jnp.float32).astype(jnp.bfloat16)
        grad_heads = grad_att.astype(jnp.float32).reshape(spans, SPAN, HEADS, HDIM)
        grad_probs = jnp.einsum('cqhd,ckhd->chqk', grad_heads, value_heads)
        row_delta = jnp.sum(prob_full * grad_probs, axis=-1, keepdims=True)
        grad_scores = (prob_full * (grad_probs - row_delta) * inv_scale).astype(jnp.bfloat16).astype(jnp.float32)
        grad_q = jnp.einsum('chqk,ckhd->cqhd', grad_scores, key_heads).astype(jnp.bfloat16).reshape(TOKENS, HID)
        grad_k = jnp.einsum('chqk,cqhd->ckhd', grad_scores, query_heads).astype(jnp.bfloat16).reshape(MROWS, HID)
        grad_v = jnp.einsum('chqk,cqhd->ckhd', prob_half.astype(jnp.float32), grad_heads).astype(jnp.bfloat16).reshape(MROWS, HID)
        accum_total = grad_in.astype(jnp.float32)
        for group_index in range(N_TENSOR):
            lower = group_index * group_width
            head_piece = jnp.dot(grad_q[:, lower:lower + group_width], w_query[section_index][:, lower:lower + group_width].T, preferred_element_type=jnp.float32)
            head_piece = lax.optimization_barrier(head_piece.astype(jnp.bfloat16))
            accum_total = accum_total + head_piece.astype(jnp.float32)
        new_grad = accum_total.astype(jnp.bfloat16)
        query_list[section_index] = jnp.dot(streams_in[section_index].T, grad_q, preferred_element_type=jnp.float32).astype(jnp.bfloat16)
        grad_key = jnp.dot(neighbours.T, grad_k, preferred_element_type=jnp.float32).astype(jnp.bfloat16)
        grad_value = jnp.dot(neighbours.T, grad_v, preferred_element_type=jnp.float32).astype(jnp.bfloat16)
        pair_list[section_index] = jnp.stack([grad_key, grad_value], axis=1)
        outer_list[section_index] = jnp.dot(attended.T, grad_in, preferred_element_type=jnp.float32).astype(jnp.bfloat16)
        neighbour_total = neighbour_total + jnp.dot(grad_k, w_key_value[section_index][:, 0].T, preferred_element_type=jnp.float32)
        neighbour_total = neighbour_total + jnp.dot(grad_v, w_key_value[section_index][:, 1].T, preferred_element_type=jnp.float32)
        stream_list[section_index] = new_grad
        grad_in = new_grad
    return (jnp.stack(stream_list), neighbour_total.astype(jnp.bfloat16), jnp.stack(query_list), jnp.stack(pair_list), jnp.stack(outer_list))
```

```python
import functools

import jax
import jax.numpy as jnp
from jax import lax
from jax.experimental import pallas as pl
from jax.experimental.pallas import tpu as pltpu
from jax.sharding import PartitionSpec as P

HDIM = 128
SPAN = 64
NTOK = 128
ROWS = 16
SCALE = HDIM ** (-0.5)
MESH = pl.DeviceIdType.MESH


def contract_rows(left, right):
    return lax.dot_general(
        left, right, (((0,), (0,)), ((), ())), preferred_element_type=jnp.float32
    )


def contract_cols(left, right):
    return lax.dot_general(
        left, right, (((1,), (1,)), ((), ())), preferred_element_type=jnp.float32
    )


def wait_bytes(ref, sem):
    pltpu.make_async_copy(ref, ref, sem).wait()


def chain_kernel(
    n_section,
    n_tensor,
    n_dp,
    cot_ref,
    q_ref,
    k_ref,
    v_ref,
    wq_ref,
    wo_ref,
    streams_out,
    grad_out,
    dq_out,
    rows_out,
    g_ref,
    dq_ref,
    att_part,
    att_recv,
    part,
    part_own,
    part_recv,
    new_ref,
    rows_ref,
    streams_ref,
    probs,
    half,
    gatt,
    gscore,
    copy_sem,
    att_send,
    att_sem,
    dq_send,
    dq_sem,
    part_send,
    part_sem,
    g_send,
    g_sem,
    rows_send,
    rows_sem,
    stream_send,
    stream_sem,
):
    sec = lax.axis_index("section")
    ten = lax.axis_index("tensor")
    dpp = lax.axis_index("dp")
    chunks = g_ref.shape[1]
    width = g_ref.shape[3]
    cols = width // n_tensor
    feats = q_ref.shape[1]
    heads = feats // HDIM
    tokens = q_ref.shape[0]
    spans = tokens // SPAN
    mrows = k_ref.shape[0]
    per_span = SPAN // ROWS

    def dp_peer(r):
        return lax.rem(dpp + r, n_dp)

    def ten_peer(r):
        return lax.rem(ten + r, n_tensor)

    barrier = pltpu.get_barrier_semaphore()
    for r in range(1, n_dp):
        pl.semaphore_signal(barrier, inc=1, device_id={"dp": dp_peer(r)}, device_id_type=MESH)
    for r in range(1, n_tensor):
        pl.semaphore_signal(barrier, inc=1, device_id={"tensor": ten_peer(r)}, device_id_type=MESH)

    @pl.when(sec > 0)
    def _():
        for r in range(n_tensor):
            pl.semaphore_signal(
                barrier, inc=1, device_id={"section": sec - 1, "tensor": ten_peer(r)}, device_id_type=MESH
            )

    @pl.when(sec < n_section - 1)
    def _():
        for r in range(n_tensor):
            pl.semaphore_signal(
                barrier, inc=1, device_id={"section": sec + 1, "tensor": ten_peer(r)}, device_id_type=MESH
            )

    @pl.when(sec == n_section - 1)
    def _():
        pltpu.make_async_copy(cot_ref, g_ref, copy_sem.at[0]).start()

    for sp in range(spans):
        for h in range(heads):
            lanes = slice(h * HDIM, (h + 1) * HDIM)
            rows = slice(sp * SPAN, (sp + 1) * SPAN)
            nrows = slice(sp * NTOK, (sp + 1) * NTOK)
            scores = contract_cols(q_ref[rows, lanes], k_ref[nrows, lanes]) * SCALE
            expo = jnp.exp(scores - jnp.max(scores, axis=-1, keepdims=True))
            prob = expo / jnp.sum(expo, axis=-1, keepdims=True)
            prob_half = prob.astype(jnp.bfloat16)
            probs[h, rows, :] = prob
            half[h, rows, :] = prob_half
            attended = jnp.dot(
                prob_half, v_ref[nrows, lanes], preferred_element_type=jnp.float32
            )
            rows_ref[dpp, rows, lanes] = attended.astype(jnp.bfloat16)

    edge = jnp.where(sec > 0, n_tensor, 0) + jnp.where(sec < n_section - 1, n_tensor, 0)
    pl.semaphore_wait(barrier, n_dp - 1 + n_tensor - 1 + edge)

    @pl.when(sec == n_section - 1)
    def _():
        pltpu.make_async_copy(cot_ref, g_ref, copy_sem.at[0]).wait()

    def stage_a(c):
        @pl.when(sec < n_section - 1)
        def _():
            wait_bytes(g_ref.at[:, c], g_sem.at[c])

        rows = g_ref[:, c].reshape(n_dp * ROWS, width)
        out = contract_cols(rows, wo_ref[...])
        att_part[c] = out.reshape(n_dp, ROWS, feats).astype(jnp.bfloat16)
        for r in range(1, n_dp):
            pltpu.make_async_remote_copy(
                src_ref=att_part.at[c, dp_peer(r)],
                dst_ref=att_recv.at[c, r - 1],
                send_sem=att_send.at[c],
                recv_sem=att_sem.at[c],
                device_id={"dp": dp_peer(r)},
                device_id_type=MESH,
            ).start()

    def stage_b(c):
        wait_bytes(att_recv.at[c], att_sem.at[c])
        total = att_part[c, dpp].astype(jnp.float32)
        for r in range(1, n_dp):
            total = total + att_recv[c, r - 1].astype(jnp.float32)
        grad = total.astype(jnp.bfloat16)
        here = pl.ds(pl.multiple_of(c * ROWS, ROWS), ROWS)
        there = pl.ds(pl.multiple_of((c // per_span) * NTOK, NTOK), NTOK)
        gatt[here, :] = grad
        for h in range(heads):
            lanes = slice(h * HDIM, (h + 1) * HDIM)
            grad_probs = contract_cols(grad[:, lanes], v_ref[there, lanes])
            prob = probs[h, here, :]
            delta = jnp.sum(prob * grad_probs, axis=-1, keepdims=True)
            grad_scores = (prob * (grad_probs - delta) * SCALE).astype(jnp.bfloat16)
            gscore[h, here, :] = grad_scores
            dq = jnp.dot(grad_scores, k_ref[there, lanes], preferred_element_type=jnp.float32)
            dq_ref[dpp, c, :, lanes] = dq.astype(jnp.bfloat16)
        for r in range(1, n_dp):
            pltpu.make_async_remote_copy(
                src_ref=dq_ref.at[dpp, c],
                dst_ref=dq_ref.at[dpp, c],
                send_sem=dq_send.at[c],
                recv_sem=dq_sem.at[c],
                device_id={"dp": dp_peer(r)},
                device_id_type=MESH,
            ).start()

    def stage_c(c):
        wait_bytes(att_recv.at[c], dq_sem.at[c])
        rows = dq_ref[:, c].reshape(n_dp * ROWS, feats)
        for r in list(range(1, n_tensor)) + [0]:
            peer = ten_peer(r)
            weight = wq_ref[pl.ds(pl.multiple_of(peer * cols, cols), cols), :]
            out = contract_cols(rows, weight).reshape(n_dp, ROWS, cols)
            if r == 0:
                part_own[c] = out
            else:
                part[c, r - 1] = out.astype(jnp.bfloat16)
                pltpu.make_async_remote_copy(
                    src_ref=part.at[c, r - 1],
                    dst_ref=part_recv.at[c, r - 1],
                    send_sem=part_send.at[c],
                    recv_sem=part_sem.at[c],
                    device_id={"tensor": peer},
                    device_id_type=MESH,
                ).start()

    def stage_d(c):
        wait_bytes(part_recv.at[c], part_sem.at[c])
        mine = pl.ds(pl.multiple_of(ten * cols, cols), cols)
        total = g_ref[:, c, :, mine].astype(jnp.float32) + part_own[c]
        for r in range(1, n_tensor):
            total = total + part_recv[c, r - 1].astype(jnp.float32)
        new_ref[:, c] = total.astype(jnp.bfloat16)

        @pl.when(sec > 0)
        def _():
            for r in range(n_tensor):
                pltpu.make_async_remote_copy(
                    src_ref=new_ref.at[:, c],
                    dst_ref=g_ref.at[:, c, :, mine],
                    send_sem=g_send.at[c],
                    recv_sem=g_sem.at[c],
                    device_id={"section": sec - 1, "tensor": ten_peer(r)},
                    device_id_type=MESH,
                ).start()

    def tick(t, carry):
        @pl.when(t < chunks)
        def _():
            stage_a(t)

        @pl.when(t > 0)
        def _():
            stage_c(t - 1)

        @pl.when(t < chunks)
        def _():
            stage_b(t)

        @pl.when(t > 0)
        def _():
            stage_d(t - 1)

        return carry

    lax.fori_loop(0, chunks + 1, tick, 0)

    for sp in range(spans):
        for h in range(heads):
            lanes = slice(h * HDIM, (h + 1) * HDIM)
            rows = slice(sp * SPAN, (sp + 1) * SPAN)
            low = tokens + sp * NTOK
            grad_k = contract_rows(gscore[h, rows, :], q_ref[rows, lanes])
            rows_ref[dpp, low : low + NTOK, lanes] = grad_k.astype(jnp.bfloat16)
            grad_v = contract_rows(half[h, rows, :], gatt[rows, lanes])
            rows_ref[dpp, low + mrows : low + mrows + NTOK, lanes] = grad_v.astype(jnp.bfloat16)
    for r in range(1, n_dp):
        pltpu.make_async_remote_copy(
            src_ref=rows_ref.at[dpp],
            dst_ref=rows_ref.at[dpp],
            send_sem=rows_send,
            recv_sem=rows_sem,
            device_id={"dp": dp_peer(r)},
            device_id_type=MESH,
        ).start()

    group = streams_ref.shape[0]
    halves = chunks // group
    mine = pl.ds(pl.multiple_of(ten * cols, cols), cols)

    def stream_block(owner):
        return new_ref.at[owner // halves, pl.ds(lax.rem(owner, halves) * group, group)]

    for r in range(1, n_tensor):
        pltpu.make_async_remote_copy(
            src_ref=stream_block(ten_peer(r)),
            dst_ref=streams_ref.at[:, :, mine],
            send_sem=stream_send,
            recv_sem=stream_sem,
            device_id={"tensor": ten_peer(r)},
            device_id_type=MESH,
        ).start()
    keep = pltpu.make_async_copy(stream_block(ten), streams_ref.at[:, :, mine], copy_sem.at[0])
    keep.start()
    outs = [
        pltpu.make_async_copy(g_ref, grad_out, copy_sem.at[1]),
        pltpu.make_async_copy(dq_ref, dq_out, copy_sem.at[2]),
        pltpu.make_async_copy(streams_ref, streams_out, copy_sem.at[3]),
        pltpu.make_async_copy(rows_ref, rows_out, copy_sem.at[4]),
    ]
    outs[0].start()
    outs[1].start()
    keep.wait()
    wait_bytes(part_recv.at[0], stream_sem)
    outs[2].start()
    wait_bytes(rows_ref.at[pl.ds(0, n_dp - 1)], rows_sem)
    outs[3].start()

    def drain(c, carry):
        wait_bytes(att_recv.at[c], att_send.at[c])
        wait_bytes(att_recv.at[c], dq_send.at[c])
        wait_bytes(part_recv.at[c], part_send.at[c])

        @pl.when(sec > 0)
        def _():
            wait_bytes(g_ref.at[:, c], g_send.at[c])

        return carry

    lax.fori_loop(0, chunks, drain, 0)
    wait_bytes(part_recv.at[0], stream_send)
    wait_bytes(rows_ref.at[pl.ds(0, n_dp - 1)], rows_send)
    for out in outs:
        out.wait()


def run_chain(cotangent, queries, keys, values, weight_query, weight_out):
    n_section = lax.axis_size("section")
    n_tensor = lax.axis_size("tensor")
    n_dp = lax.axis_size("dp")
    total, width = cotangent.shape
    tokens, feats = queries.shape
    mrows = keys.shape[0]
    heads = feats // HDIM
    chunks = tokens // ROWS
    cols = width // n_tensor
    held = tokens + 2 * mrows
    group = total // n_tensor // ROWS
    bf16, f32 = jnp.bfloat16, jnp.float32
    vmem = pl.BlockSpec(memory_space=pltpu.VMEM)
    anywhere = pl.BlockSpec(memory_space=pl.ANY)
    dma = pltpu.SemaphoreType.DMA
    streams, grad, dq, rows = pl.pallas_call(
        functools.partial(chain_kernel, n_section, n_tensor, n_dp),
        out_shape=[
            jax.ShapeDtypeStruct((group, ROWS, width), bf16),
            jax.ShapeDtypeStruct((n_dp, chunks, ROWS, width), bf16),
            jax.ShapeDtypeStruct((n_dp, chunks, ROWS, feats), bf16),
            jax.ShapeDtypeStruct((n_dp, held, feats), bf16),
        ],
        in_specs=[anywhere] + [vmem] * 5,
        out_specs=[anywhere] * 4,
        scratch_shapes=[
            pltpu.VMEM((n_dp, chunks, ROWS, width), bf16),
            pltpu.VMEM((n_dp, chunks, ROWS, feats), bf16),
            pltpu.VMEM((chunks, n_dp, ROWS, feats), bf16),
            pltpu.VMEM((chunks, n_dp - 1, ROWS, feats), bf16),
            pltpu.VMEM((chunks, n_tensor - 1, n_dp, ROWS, cols), bf16),
            pltpu.VMEM((chunks, n_dp, ROWS, cols), f32),
            pltpu.VMEM((chunks, n_tensor - 1, n_dp, ROWS, cols), bf16),
            pltpu.VMEM((n_dp, chunks, ROWS, cols), bf16),
            pltpu.VMEM((n_dp, held, feats), bf16),
            pltpu.VMEM((group, ROWS, width), bf16),
            pltpu.VMEM((heads, tokens, NTOK), f32),
            pltpu.VMEM((heads, tokens, NTOK), bf16),
            pltpu.VMEM((tokens, feats), bf16),
            pltpu.VMEM((heads, tokens, NTOK), bf16),
            dma((5,)),
            dma((chunks,)),
            dma((chunks,)),
            dma((chunks,)),
            dma((chunks,)),
            dma((chunks,)),
            dma((chunks,)),
            dma((chunks,)),
            dma((chunks,)),
            dma,
            dma,
            dma,
            dma,
        ],
        compiler_params=pltpu.CompilerParams(
            collective_id=0, has_side_effects=True, vmem_limit_bytes=48 * 2**20
        ),
    )(
        cotangent.reshape(n_dp, chunks, ROWS, width),
        queries,
        keys,
        values,
        weight_query,
        weight_out,
    )
    rows = [
        rows[:, low : low + size].reshape(n_dp * size, feats)
        for low, size in ((0, tokens), (tokens, mrows), (tokens + mrows, mrows))
    ]
    return (
        streams.reshape(-1, width),
        grad.reshape(total, width),
        dq.reshape(total, feats),
        rows,
    )


def on_device(cotangent, queries, keys_values, streams_in, neighbours, w_query, w_key_value, w_out):
    weight_key = w_key_value[0][:, 0]
    weight_value = w_key_value[0][:, 1]
    streams, grad, dq, (attended, grad_k, grad_v) = run_chain(
        cotangent, queries[0], keys_values[0][:, 0], keys_values[0][:, 1], w_query[0], w_out[0]
    )
    neighbour_term = contract_cols(grad_k, weight_key) + contract_cols(grad_v, weight_value)
    neighbour_part = lax.psum_scatter(
        neighbour_term.astype(jnp.bfloat16), ("section", "tensor"), scatter_dimension=0, tiled=True
    )
    grad_query = contract_rows(streams_in[0], dq).astype(jnp.bfloat16)
    grad_key = contract_rows(neighbours, grad_k).astype(jnp.bfloat16)
    grad_value = contract_rows(neighbours, grad_v).astype(jnp.bfloat16)
    grad_pair = jnp.stack([grad_key, grad_value], axis=1)
    grad_out = contract_rows(attended, grad).astype(jnp.bfloat16)
    return (streams[None], neighbour_part, grad_query[None], grad_pair[None], grad_out[None])


def solution(mesh):
    in_specs = (
        P(None, "dp"),
        P("section", "dp", "tensor"),
        P("section", "dp", None, "tensor"),
        P("section", None, "dp"),
        P(None, "dp"),
        P("section", "dp", "tensor"),
        P("section", "dp", None, "tensor"),
        P("section", "tensor", "dp"),
    )
    out_specs = (
        P("section", "tensor", "dp"),
        P(("section", "tensor"), "dp"),
        P("section", "dp", "tensor"),
        P("section", "dp", None, "tensor"),
        P("section", "tensor", "dp"),
    )
    return jax.shard_map(
        on_device, mesh=mesh, in_specs=in_specs, out_specs=out_specs, check_vma=False
    )
```

```python
import functools

import jax
import jax.numpy as jnp
from jax import lax
from jax.experimental import pallas as pl
from jax.experimental.pallas import tpu as pltpu
from jax.sharding import PartitionSpec as P

HDIM = 128
SPAN = 64
NTOK = 128
SCALE = HDIM ** (-0.5)
MESH = pl.DeviceIdType.MESH


def contract_rows(left, right):
    return lax.dot_general(
        left, right, (((0,), (0,)), ((), ())), preferred_element_type=jnp.float32
    )


def contract_cols(left, right):
    return lax.dot_general(
        left, right, (((1,), (1,)), ((), ())), preferred_element_type=jnp.float32
    )


def wait_bytes(ref, sem):
    pltpu.make_async_copy(ref, ref, sem).wait()


def chain_kernel(
    n_section,
    n_tensor,
    n_dp,
    cot_ref,
    q_ref,
    k_ref,
    v_ref,
    wq_ref,
    wo_ref,
    streams_out,
    grad_out,
    dq_out,
    att_out,
    dk_out,
    dv_out,
    g_ref,
    qkv,
    pair_part,
    pair_recv,
    z_part,
    z_recv,
    part,
    part_own,
    part_recv,
    new_ref,
    streams_ref,
    dq_ref,
    att_ref,
    dk_ref,
    dv_ref,
    probs,
    half,
    gatt,
    gscore,
    copy_sem,
    qkv_send,
    qkv_sem,
    pair_send,
    pair_sem,
    z_send,
    z_sem,
    part_send,
    part_sem,
    g_send,
    g_sem,
    stream_send,
    stream_sem,
):
    sec = lax.axis_index("section")
    ten = lax.axis_index("tensor")
    dpp = lax.axis_index("dp")
    width = g_ref.shape[1]
    spans = g_ref.shape[0] // SPAN
    owned = spans // n_dp
    cols = width // n_tensor
    feats = q_ref.shape[1]
    heads = feats // HDIM
    mine = pl.ds(pl.multiple_of(ten * cols, cols), cols)
    sibling = dpp + 1 - 2 * lax.rem(dpp, 2)
    across = lax.rem(dpp + 2, n_dp)

    def dp_peer(r):
        return lax.rem(dpp + r, n_dp)

    def ten_peer(r):
        return lax.rem(ten + r, n_tensor)

    def span_at(t):
        return lax.rem(t + owned, spans)

    def token_rows(c):
        return pl.ds(pl.multiple_of(c * SPAN, SPAN), SPAN)

    def pair_rows(c):
        return pl.ds(pl.multiple_of(c * NTOK, NTOK), NTOK)

    def send(src, dst, send_sem, recv_sem, device):
        pltpu.make_async_remote_copy(
            src_ref=src,
            dst_ref=dst,
            send_sem=send_sem,
            recv_sem=recv_sem,
            device_id=device,
            device_id_type=MESH,
        ).start()

    barrier = pltpu.get_barrier_semaphore()
    for r in range(1, n_dp):
        pl.semaphore_signal(barrier, inc=1, device_id={"dp": dp_peer(r)}, device_id_type=MESH)
    for r in range(1, n_tensor):
        pl.semaphore_signal(barrier, inc=1, device_id={"tensor": ten_peer(r)}, device_id_type=MESH)

    @pl.when(sec > 0)
    def _():
        for r in range(n_tensor):
            pl.semaphore_signal(
                barrier, inc=1, device_id={"section": sec - 1, "tensor": ten_peer(r)}, device_id_type=MESH
            )

    @pl.when(sec < n_section - 1)
    def _():
        for r in range(n_tensor):
            pl.semaphore_signal(
                barrier, inc=1, device_id={"section": sec + 1, "tensor": ten_peer(r)}, device_id_type=MESH
            )

    @pl.when(sec == n_section - 1)
    def _():
        pltpu.make_async_copy(cot_ref, g_ref, copy_sem.at[0]).start()

    for i in range(owned):
        block = qkv.at[dpp * owned + i]
        block[0:SPAN, :] = q_ref[i * SPAN : (i + 1) * SPAN, :]
        block[SPAN : SPAN + NTOK, :] = k_ref[i * NTOK : (i + 1) * NTOK, :]
        block[SPAN + NTOK : SPAN + 2 * NTOK, :] = v_ref[i * NTOK : (i + 1) * NTOK, :]

    edge = jnp.where(sec > 0, n_tensor, 0) + jnp.where(sec < n_section - 1, n_tensor, 0)
    pl.semaphore_wait(barrier, n_dp - 1 + n_tensor - 1 + edge)

    @pl.when(sec == n_section - 1)
    def _():
        pltpu.make_async_copy(cot_ref, g_ref, copy_sem.at[0]).wait()

    key_rows = slice(SPAN, SPAN + NTOK)
    value_rows = slice(SPAN + NTOK, SPAN + 2 * NTOK)

    def head_lanes(h):
        return slice(h * HDIM, (h + 1) * HDIM)

    def share(t):
        c = span_at(t)

        @pl.when(c // owned == dpp)
        def _():
            for r in range(1, n_dp):
                send(qkv.at[c], qkv.at[c], qkv_send.at[c], qkv_sem.at[c], {"dp": dp_peer(r)})

    def stage_a(t):
        c = span_at(t)

        @pl.when(sec < n_section - 1)
        def _():
            wait_bytes(g_ref.at[token_rows(c)], g_sem.at[c])

        out = contract_cols(g_ref[token_rows(c), :], wo_ref[...])
        pair_part[c] = out.astype(jnp.bfloat16)
        send(pair_part.at[c], pair_recv.at[c], pair_send.at[c], pair_sem.at[c], {"dp": sibling})

    def stage_a2(t):
        c = span_at(t)
        wait_bytes(pair_recv.at[c], pair_sem.at[c])
        total = pair_part[c].astype(jnp.float32) + pair_recv[c].astype(jnp.float32)
        z_part[c] = total.astype(jnp.bfloat16)
        send(z_part.at[c], z_recv.at[c], z_send.at[c], z_sem.at[c], {"dp": across})

    def stage_p(t):
        c = span_at(t)

        @pl.when(c // owned != dpp)
        def _():
            wait_bytes(qkv.at[c], qkv_sem.at[c])

        for h in range(heads):
            lanes = head_lanes(h)
            scores = contract_cols(qkv[c, 0:SPAN, lanes], qkv[c, key_rows, lanes]) * SCALE
            expo = jnp.exp(scores - jnp.max(scores, axis=-1, keepdims=True))
            prob = expo / jnp.sum(expo, axis=-1, keepdims=True)
            prob_half = prob.astype(jnp.bfloat16)
            probs[c, h] = prob
            half[c, h] = prob_half
            attended = jnp.dot(
                prob_half, qkv[c, value_rows, lanes], preferred_element_type=jnp.float32
            )
            att_ref[token_rows(c), lanes] = attended.astype(jnp.bfloat16)

    def stage_bc(t):
        c = span_at(t)
        wait_bytes(z_recv.at[c], z_sem.at[c])
        total = z_part[c].astype(jnp.float32) + z_recv[c].astype(jnp.float32)
        grad = total.astype(jnp.bfloat16)
        gatt[c] = grad
        for h in range(heads):
            lanes = head_lanes(h)
            grad_probs = contract_cols(grad[:, lanes], qkv[c, value_rows, lanes])
            prob = probs[c, h]
            delta = jnp.sum(prob * grad_probs, axis=-1, keepdims=True)
            grad_scores = (prob * (grad_probs - delta) * SCALE).astype(jnp.bfloat16)
            gscore[c, h] = grad_scores
            dq = jnp.dot(grad_scores, qkv[c, key_rows, lanes], preferred_element_type=jnp.float32)
            dq_ref[token_rows(c), lanes] = dq.astype(jnp.bfloat16)
        rows = dq_ref[token_rows(c), :]
        for r in list(range(1, n_tensor)) + [0]:
            peer = ten_peer(r)
            weight = wq_ref[pl.ds(pl.multiple_of(peer * cols, cols), cols), :]
            out = contract_cols(rows, weight)
            if r == 0:
                part_own[c] = out
            else:
                part[c, r - 1] = out.astype(jnp.bfloat16)
                send(
                    part.at[c, r - 1],
                    part_recv.at[c, r - 1],
                    part_send.at[c],
                    part_sem.at[c],
                    {"tensor": peer},
                )

    def stage_d(t):
        c = span_at(t)
        wait_bytes(part_recv.at[c], part_sem.at[c])
        total = g_ref[token_rows(c), mine].astype(jnp.float32) + part_own[c]
        for r in range(1, n_tensor):
            total = total + part_recv[c, r - 1].astype(jnp.float32)
        new_ref[c] = total.astype(jnp.bfloat16)

        @pl.when(sec > 0)
        def _():
            for r in range(n_tensor):
                send(
                    new_ref.at[c],
                    g_ref.at[token_rows(c), mine],
                    g_send.at[c],
                    g_sem.at[c],
                    {"section": sec - 1, "tensor": ten_peer(r)},
                )

        @pl.when(c != ten)
        def _():
            send(new_ref.at[c], streams_ref.at[:, mine], stream_send.at[c], stream_sem, {"tensor": c})

        @pl.when(c == ten)
        def _():
            streams_ref[:, mine] = new_ref[c]

    def stage_k(t):
        c = span_at(t)
        for h in range(heads):
            lanes = head_lanes(h)
            grad_k = contract_rows(gscore[c, h], qkv[c, 0:SPAN, lanes])
            dk_ref[pair_rows(c), lanes] = grad_k.astype(jnp.bfloat16)
            grad_v = contract_rows(half[c, h], gatt[c, :, lanes])
            dv_ref[pair_rows(c), lanes] = grad_v.astype(jnp.bfloat16)

    def tick(t, carry):
        first = t < spans
        second = jnp.logical_and(t > 0, t <= spans)

        @pl.when(second)
        def _():
            stage_bc(t - 1)

        @pl.when(first)
        def _():
            share(t)
            stage_a(t)

        @pl.when(second)
        def _():
            stage_k(t - 1)

        @pl.when(first)
        def _():
            stage_a2(t)

        @pl.when(t > 1)
        def _():
            stage_d(t - 2)

        @pl.when(first)
        def _():
            stage_p(t)

        return carry

    lax.fori_loop(0, spans + 2, tick, 0)

    outs = [
        pltpu.make_async_copy(g_ref, grad_out, copy_sem.at[0]),
        pltpu.make_async_copy(dq_ref, dq_out, copy_sem.at[1]),
        pltpu.make_async_copy(att_ref, att_out, copy_sem.at[2]),
        pltpu.make_async_copy(dk_ref, dk_out, copy_sem.at[3]),
        pltpu.make_async_copy(dv_ref, dv_out, copy_sem.at[4]),
        pltpu.make_async_copy(streams_ref, streams_out, copy_sem.at[5]),
    ]
    for out in outs[:-1]:
        out.start()
    wait_bytes(part_recv.at[0], stream_sem)
    outs[-1].start()

    def drain(c, carry):
        wait_bytes(pair_recv.at[c], pair_send.at[c])
        wait_bytes(z_recv.at[c], z_send.at[c])
        wait_bytes(part_recv.at[c], part_send.at[c])

        @pl.when(c // owned == dpp)
        def _():
            wait_bytes(qkv.at[pl.ds(0, n_dp - 1)], qkv_send.at[c])

        @pl.when(sec > 0)
        def _():
            wait_bytes(g_ref.at[token_rows(c)], g_send.at[c])

        @pl.when(c != ten)
        def _():
            wait_bytes(new_ref.at[c], stream_send.at[c])

        return carry

    lax.fori_loop(0, spans, drain, 0)
    for out in outs:
        out.wait()


def run_chain(cotangent, queries, keys, values, weight_query, weight_out):
    n_section = lax.axis_size("section")
    n_tensor = lax.axis_size("tensor")
    n_dp = lax.axis_size("dp")
    total, width = cotangent.shape
    feats = queries.shape[1]
    mrows = keys.shape[0] * n_dp
    heads = feats // HDIM
    spans = total // SPAN
    cols = width // n_tensor
    bf16, f32 = jnp.bfloat16, jnp.float32
    vmem = pl.BlockSpec(memory_space=pltpu.VMEM)
    anywhere = pl.BlockSpec(memory_space=pl.ANY)
    dma = pltpu.SemaphoreType.DMA
    return pl.pallas_call(
        functools.partial(chain_kernel, n_section, n_tensor, n_dp),
        out_shape=[
            jax.ShapeDtypeStruct((SPAN, width), bf16),
            jax.ShapeDtypeStruct((total, width), bf16),
            jax.ShapeDtypeStruct((total, feats), bf16),
            jax.ShapeDtypeStruct((total, feats), bf16),
            jax.ShapeDtypeStruct((mrows, feats), bf16),
            jax.ShapeDtypeStruct((mrows, feats), bf16),
        ],
        in_specs=[anywhere] + [vmem] * 5,
        out_specs=[anywhere] * 6,
        scratch_shapes=[
            pltpu.VMEM((total, width), bf16),
            pltpu.VMEM((spans, SPAN + 2 * NTOK, feats), bf16),
            pltpu.VMEM((spans, SPAN, feats), bf16),
            pltpu.VMEM((spans, SPAN, feats), bf16),
            pltpu.VMEM((spans, SPAN, feats), bf16),
            pltpu.VMEM((spans, SPAN, feats), bf16),
            pltpu.VMEM((spans, n_tensor - 1, SPAN, cols), bf16),
            pltpu.VMEM((spans, SPAN, cols), f32),
            pltpu.VMEM((spans, n_tensor - 1, SPAN, cols), bf16),
            pltpu.VMEM((spans, SPAN, cols), bf16),
            pltpu.VMEM((SPAN, width), bf16),
            pltpu.VMEM((total, feats), bf16),
            pltpu.VMEM((total, feats), bf16),
            pltpu.VMEM((mrows, feats), bf16),
            pltpu.VMEM((mrows, feats), bf16),
            pltpu.VMEM((spans, heads, SPAN, NTOK), f32),
            pltpu.VMEM((spans, heads, SPAN, NTOK), bf16),
            pltpu.VMEM((spans, SPAN, feats), bf16),
            pltpu.VMEM((spans, heads, SPAN, NTOK), bf16),
            dma((6,)),
            dma((spans,)),
            dma((spans,)),
            dma((spans,)),
            dma((spans,)),
            dma((spans,)),
            dma((spans,)),
            dma((spans,)),
            dma((spans,)),
            dma((spans,)),
            dma((spans,)),
            dma((spans,)),
            dma,
        ],
        compiler_params=pltpu.CompilerParams(
            collective_id=0, has_side_effects=True, vmem_limit_bytes=48 * 2**20
        ),
    )(cotangent, queries, keys, values, weight_query, weight_out)


def on_device(cotangent, queries, keys_values, streams_in, neighbours, w_query, w_key_value, w_out):
    weight_key = w_key_value[0][:, 0]
    weight_value = w_key_value[0][:, 1]
    streams, grad, dq, attended, grad_k, grad_v = run_chain(
        cotangent, queries[0], keys_values[0][:, 0], keys_values[0][:, 1], w_query[0], w_out[0]
    )
    neighbour_term = contract_cols(grad_k, weight_key) + contract_cols(grad_v, weight_value)
    neighbour_part = lax.psum_scatter(
        neighbour_term.astype(jnp.bfloat16), ("section", "tensor"), scatter_dimension=0, tiled=True
    )
    grad_query = contract_rows(streams_in[0], dq).astype(jnp.bfloat16)
    grad_key = contract_rows(neighbours, grad_k).astype(jnp.bfloat16)
    grad_value = contract_rows(neighbours, grad_v).astype(jnp.bfloat16)
    grad_pair = jnp.stack([grad_key, grad_value], axis=1)
    grad_out = contract_rows(attended, grad).astype(jnp.bfloat16)
    return (streams[None], neighbour_part, grad_query[None], grad_pair[None], grad_out[None])


def solution(mesh):
    in_specs = (
        P(None, "dp"),
        P("section", "dp", "tensor"),
        P("section", "dp", None, "tensor"),
        P("section", None, "dp"),
        P(None, "dp"),
        P("section", "dp", "tensor"),
        P("section", "dp", None, "tensor"),
        P("section", "tensor", "dp"),
    )
    out_specs = (
        P("section", "tensor", "dp"),
        P(("section", "tensor"), "dp"),
        P("section", "dp", "tensor"),
        P("section", "dp", None, "tensor"),
        P("section", "tensor", "dp"),
    )
    return jax.shard_map(
        on_device, mesh=mesh, in_specs=in_specs, out_specs=out_specs, check_vma=False
    )
```

```python
import functools

import jax
import jax.numpy as jnp
from jax import lax
from jax.experimental import pallas as pl
from jax.experimental.pallas import tpu as pltpu
from jax.sharding import PartitionSpec as P

HDIM = 128
SPAN = 64
NTOK = 128
SCALE = HDIM ** (-0.5)
MESH = pl.DeviceIdType.MESH


def contract_rows(left, right):
    return lax.dot_general(
        left, right, (((0,), (0,)), ((), ())), preferred_element_type=jnp.float32
    )


def contract_cols(left, right):
    return lax.dot_general(
        left, right, (((1,), (1,)), ((), ())), preferred_element_type=jnp.float32
    )


def wait_bytes(ref, sem):
    pltpu.make_async_copy(ref, ref, sem).wait()


def chain_kernel(
    n_section,
    n_tensor,
    n_dp,
    cot_ref,
    q_ref,
    k_ref,
    v_ref,
    wq_hbm,
    wo_ref,
    wk_hbm,
    wv_hbm,
    streams_out,
    near_out,
    grad_out,
    dq_out,
    att_out,
    dk_out,
    dv_out,
    g_ref,
    qkv,
    pair_part,
    pair_recv,
    z_part,
    z_recv,
    part,
    part_own,
    part_recv,
    new_ref,
    streams_ref,
    dq_ref,
    att_ref,
    dk_ref,
    dv_ref,
    probs,
    half,
    gatt,
    gscore,
    wq_ref,
    wk_ref,
    wv_ref,
    near_part,
    near_recv,
    sum_part,
    sum_recv,
    near_ref,
    copy_sem,
    qkv_send,
    qkv_sem,
    pair_send,
    pair_sem,
    z_send,
    z_sem,
    part_send,
    part_sem,
    g_send,
    g_sem,
    stream_send,
    stream_sem,
    near_send,
    near_sem,
    sum_send,
    sum_sem,
):
    sec = lax.axis_index("section")
    ten = lax.axis_index("tensor")
    dpp = lax.axis_index("dp")
    width = g_ref.shape[1]
    spans = g_ref.shape[0] // SPAN
    owned = spans // n_dp
    cols = width // n_tensor
    feats = q_ref.shape[1]
    heads = feats // HDIM
    mine = pl.ds(pl.multiple_of(ten * cols, cols), cols)
    sibling = dpp + 1 - 2 * lax.rem(dpp, 2)
    across = lax.rem(dpp + 2, n_dp)

    def dp_peer(r):
        return lax.rem(dpp + r, n_dp)

    def ten_peer(r):
        return lax.rem(ten + r, n_tensor)

    share_spans = spans // n_section
    weights = [
        pltpu.make_async_copy(wq_hbm, wq_ref, copy_sem.at[1]),
        pltpu.make_async_copy(wk_hbm, wk_ref, copy_sem.at[2]),
        pltpu.make_async_copy(wv_hbm, wv_ref, copy_sem.at[3]),
    ]

    def span_at(t):
        return lax.rem(t + owned, spans)

    def token_rows(c):
        return pl.ds(pl.multiple_of(c * SPAN, SPAN), SPAN)

    def pair_rows(c):
        return pl.ds(pl.multiple_of(c * NTOK, NTOK), NTOK)

    def send(src, dst, send_sem, recv_sem, device):
        pltpu.make_async_remote_copy(
            src_ref=src,
            dst_ref=dst,
            send_sem=send_sem,
            recv_sem=recv_sem,
            device_id=device,
            device_id_type=MESH,
        ).start()

    barrier = pltpu.get_barrier_semaphore()
    for r in range(1, n_dp):
        pl.semaphore_signal(barrier, inc=1, device_id={"dp": dp_peer(r)}, device_id_type=MESH)
    for r in range(1, n_tensor):
        pl.semaphore_signal(barrier, inc=1, device_id={"tensor": ten_peer(r)}, device_id_type=MESH)

    for r in range(1, n_section):
        there = lax.rem(sec + r, n_section)
        pl.semaphore_signal(barrier, inc=1, device_id={"section": there}, device_id_type=MESH)

    @pl.when(sec > 0)
    def _():
        for r in range(n_tensor):
            pl.semaphore_signal(
                barrier, inc=1, device_id={"section": sec - 1, "tensor": ten_peer(r)}, device_id_type=MESH
            )

    @pl.when(sec < n_section - 1)
    def _():
        for r in range(n_tensor):
            pl.semaphore_signal(
                barrier, inc=1, device_id={"section": sec + 1, "tensor": ten_peer(r)}, device_id_type=MESH
            )

    @pl.when(sec == n_section - 1)
    def _():
        pltpu.make_async_copy(cot_ref, g_ref, copy_sem.at[0]).start()

    for weight in weights:
        weight.start()
    for i in range(owned):
        block = qkv.at[dpp * owned + i]
        block[0:SPAN, :] = q_ref[i * SPAN : (i + 1) * SPAN, :]
        block[SPAN : SPAN + NTOK, :] = k_ref[i * NTOK : (i + 1) * NTOK, :]
        block[SPAN + NTOK : SPAN + 2 * NTOK, :] = v_ref[i * NTOK : (i + 1) * NTOK, :]

    edge = jnp.where(sec > 0, n_tensor, 0) + jnp.where(sec < n_section - 1, n_tensor, 0)
    pl.semaphore_wait(barrier, n_dp - 1 + n_tensor - 1 + n_section - 1 + edge)

    @pl.when(sec == n_section - 1)
    def _():
        pltpu.make_async_copy(cot_ref, g_ref, copy_sem.at[0]).wait()

    key_rows = slice(SPAN, SPAN + NTOK)
    value_rows = slice(SPAN + NTOK, SPAN + 2 * NTOK)

    def head_lanes(h):
        return slice(h * HDIM, (h + 1) * HDIM)

    def share(t):
        c = span_at(t)

        @pl.when(c // owned == dpp)
        def _():
            send(qkv.at[c], qkv.at[c], qkv_send.at[c], qkv_sem.at[c], {"dp": across})
            send(qkv.at[c], qkv.at[c], qkv_send.at[c], qkv_sem.at[c], {"dp": sibling})

    def relay(t):
        c = span_at(t)

        @pl.when(c // owned == across)
        def _():
            wait_bytes(qkv.at[c], qkv_sem.at[c])
            send(qkv.at[c], qkv.at[c], qkv_send.at[c], qkv_sem.at[c], {"dp": sibling})

    def stage_a(t):
        c = span_at(t)

        @pl.when(sec < n_section - 1)
        def _():
            wait_bytes(g_ref.at[token_rows(c)], g_sem.at[c])

        out = contract_cols(g_ref[token_rows(c), :], wo_ref[...])
        pair_part[c] = out.astype(jnp.bfloat16)
        send(pair_part.at[c], pair_recv.at[c], pair_send.at[c], pair_sem.at[c], {"dp": sibling})

    def stage_a2(t):
        c = span_at(t)
        wait_bytes(pair_recv.at[c], pair_sem.at[c])
        total = pair_part[c].astype(jnp.float32) + pair_recv[c].astype(jnp.float32)
        z_part[c] = total.astype(jnp.bfloat16)
        send(z_part.at[c], z_recv.at[c], z_send.at[c], z_sem.at[c], {"dp": across})

    def stage_p(t):
        c = span_at(t)

        @pl.when(jnp.logical_and(c // owned != dpp, c // owned != across))
        def _():
            wait_bytes(qkv.at[c], qkv_sem.at[c])

        for h in range(heads):
            lanes = head_lanes(h)
            scores = contract_cols(qkv[c, 0:SPAN, lanes], qkv[c, key_rows, lanes]) * SCALE
            expo = jnp.exp(scores - jnp.max(scores, axis=-1, keepdims=True))
            prob = expo / jnp.sum(expo, axis=-1, keepdims=True)
            prob_half = prob.astype(jnp.bfloat16)
            probs[c, h] = prob
            half[c, h] = prob_half
            attended = jnp.dot(
                prob_half, qkv[c, value_rows, lanes], preferred_element_type=jnp.float32
            )
            att_ref[token_rows(c), lanes] = attended.astype(jnp.bfloat16)

    def stage_bc(t):
        c = span_at(t)
        wait_bytes(z_recv.at[c], z_sem.at[c])
        total = z_part[c].astype(jnp.float32) + z_recv[c].astype(jnp.float32)
        grad = total.astype(jnp.bfloat16)
        gatt[c] = grad
        for h in range(heads):
            lanes = head_lanes(h)
            grad_probs = contract_cols(grad[:, lanes], qkv[c, value_rows, lanes])
            prob = probs[c, h]
            delta = jnp.sum(prob * grad_probs, axis=-1, keepdims=True)
            grad_scores = (prob * (grad_probs - delta) * SCALE).astype(jnp.bfloat16)
            gscore[c, h] = grad_scores
            dq = jnp.dot(grad_scores, qkv[c, key_rows, lanes], preferred_element_type=jnp.float32)
            dq_ref[token_rows(c), lanes] = dq.astype(jnp.bfloat16)
        rows = dq_ref[token_rows(c), :]
        for r in list(range(1, n_tensor)) + [0]:
            peer = ten_peer(r)
            weight = wq_ref[pl.ds(pl.multiple_of(peer * cols, cols), cols), :]
            out = contract_cols(rows, weight)
            if r == 0:
                part_own[c] = out
            else:
                part[c, r - 1] = out.astype(jnp.bfloat16)
                send(
                    part.at[c, r - 1],
                    part_recv.at[c, r - 1],
                    part_send.at[c],
                    part_sem.at[c],
                    {"tensor": peer},
                )

    def stage_d(t):
        c = span_at(t)
        wait_bytes(part_recv.at[c], part_sem.at[c])
        total = g_ref[token_rows(c), mine].astype(jnp.float32) + part_own[c]
        for r in range(1, n_tensor):
            total = total + part_recv[c, r - 1].astype(jnp.float32)
        new_ref[c] = total.astype(jnp.bfloat16)

        @pl.when(sec > 0)
        def _():
            for r in range(n_tensor):
                send(
                    new_ref.at[c],
                    g_ref.at[token_rows(c), mine],
                    g_send.at[c],
                    g_sem.at[c],
                    {"section": sec - 1, "tensor": ten_peer(r)},
                )

        @pl.when(c != ten)
        def _():
            send(new_ref.at[c], streams_ref.at[:, mine], stream_send.at[c], stream_sem, {"tensor": c})

        @pl.when(c == ten)
        def _():
            streams_ref[:, mine] = new_ref[c]

    def stage_k(t):
        c = span_at(t)
        for h in range(heads):
            lanes = head_lanes(h)
            grad_k = contract_rows(gscore[c, h], qkv[c, 0:SPAN, lanes])
            dk_ref[pair_rows(c), lanes] = grad_k.astype(jnp.bfloat16)
            grad_v = contract_rows(half[c, h], gatt[c, :, lanes])
            dv_ref[pair_rows(c), lanes] = grad_v.astype(jnp.bfloat16)

    def stage_n(c):
        owner = c // share_spans
        for low in range(0, width, 512):
            block = slice(low, low + 512)
            out = contract_cols(dk_ref[pair_rows(c), :], wk_ref[block, :])
            out = out + contract_cols(dv_ref[pair_rows(c), :], wv_ref[block, :])
            near_part[c, :, block] = out.astype(jnp.bfloat16)

        @pl.when(owner != sec)
        def _():
            slot = lax.rem(sec - owner + n_section, n_section) - 1
            turn = lax.rem(c, share_spans)
            send(
                near_part.at[c],
                near_recv.at[slot, turn],
                near_send.at[c],
                near_sem.at[slot, turn],
                {"section": owner},
            )

    last = sec == n_section - 1

    @pl.when(jnp.logical_not(last))
    def _():
        lax.fori_loop(0, spans, lambda t, carry: (share(t), carry)[1], 0)
        lax.fori_loop(0, spans, lambda t, carry: (relay(t), carry)[1], 0)

    @pl.when(last)
    def _():
        share(0)
        share(1)

    def tick(t, carry):
        first = t < spans
        second = jnp.logical_and(t > 0, t <= spans)

        @pl.when(jnp.logical_and(last, jnp.logical_and(first, t > 0)))
        def _():
            relay(t)

        @pl.when(first)
        def _():
            stage_a(t)

        @pl.when(t > 1)
        def _():
            stage_k(t - 2)

        @pl.when(first)
        def _():
            stage_a2(t)

            @pl.when(jnp.logical_and(last, t == 0))
            def _():
                relay(t)

            @pl.when(jnp.logical_and(last, t < spans - 2))
            def _():
                share(t + 2)

        @pl.when(jnp.logical_and(sec == 0, t > 1))
        def _():
            stage_n(span_at(t - 2))

        @pl.when(first)
        def _():
            stage_p(t)

        @pl.when(t == 0)
        def _():
            for weight in weights:
                weight.wait()

        @pl.when(second)
        def _():
            stage_bc(t - 1)

        @pl.when(t > 1)
        def _():
            stage_d(t - 2)

        return carry

    lax.fori_loop(0, spans + 2, tick, 0)

    outs = [
        pltpu.make_async_copy(g_ref, grad_out, copy_sem.at[0]),
        pltpu.make_async_copy(dq_ref, dq_out, copy_sem.at[1]),
        pltpu.make_async_copy(att_ref, att_out, copy_sem.at[2]),
        pltpu.make_async_copy(dk_ref, dk_out, copy_sem.at[3]),
        pltpu.make_async_copy(dv_ref, dv_out, copy_sem.at[4]),
        pltpu.make_async_copy(streams_ref, streams_out, copy_sem.at[5]),
    ]
    near_copy = pltpu.make_async_copy(near_ref, near_out, copy_sem.at[6])
    for out in outs[:-1]:
        out.start()

    @pl.when(sec > 0)
    def _():
        lax.fori_loop(0, spans, lambda c, carry: (stage_n(c), carry)[1], 0)

    keep = sum_part.shape[2]
    quarter = sum_part.shape[1]

    def sum_sections(turn, carry):
        c = sec * share_spans + turn
        for slot in range(n_section - 1):
            wait_bytes(near_recv.at[slot, turn], near_sem.at[slot, turn])
        for piece in range(quarter):
            rows = slice(piece * keep, (piece + 1) * keep)
            total = near_part[c, rows, :].astype(jnp.float32)
            for slot in range(n_section - 1):
                total = total + near_recv[slot, turn, rows, :].astype(jnp.float32)
            sum_part[turn, piece] = total.astype(jnp.bfloat16)
        for step in range(quarter):
            piece = lax.rem(ten + step, quarter)
            peer = turn * quarter + piece

            @pl.when(peer != ten)
            def _():
                send(
                    sum_part.at[turn, piece],
                    sum_recv.at[lax.rem(ten - peer + n_tensor, n_tensor) - 1],
                    sum_send,
                    sum_sem,
                    {"tensor": peer},
                )

        return carry

    lax.fori_loop(0, share_spans, sum_sections, 0)
    wait_bytes(part_recv.at[0], stream_sem)
    outs[-1].start()
    wait_bytes(sum_recv, sum_sem)
    total = sum_part[ten // quarter, lax.rem(ten, quarter)].astype(jnp.float32)
    for slot in range(n_tensor - 1):
        total = total + sum_recv[slot].astype(jnp.float32)
    near_ref[...] = total.astype(jnp.bfloat16)
    near_copy.start()

    def drain(c, carry):
        wait_bytes(pair_recv.at[c], pair_send.at[c])
        wait_bytes(z_recv.at[c], z_send.at[c])
        wait_bytes(part_recv.at[c], part_send.at[c])

        @pl.when(c // owned == dpp)
        def _():
            wait_bytes(qkv.at[pl.ds(0, 2)], qkv_send.at[c])

        @pl.when(c // owned == across)
        def _():
            wait_bytes(qkv.at[c], qkv_send.at[c])

        @pl.when(c // share_spans != sec)
        def _():
            wait_bytes(near_part.at[c], near_send.at[c])

        @pl.when(sec > 0)
        def _():
            wait_bytes(g_ref.at[token_rows(c)], g_send.at[c])

        @pl.when(c != ten)
        def _():
            wait_bytes(new_ref.at[c], stream_send.at[c])

        return carry

    lax.fori_loop(0, spans, drain, 0)
    wait_bytes(sum_recv, sum_send)
    for out in outs:
        out.wait()
    near_copy.wait()


def run_chain(cotangent, queries, keys, values, weight_query, weight_out, weight_key, weight_value):
    n_section = lax.axis_size("section")
    n_tensor = lax.axis_size("tensor")
    n_dp = lax.axis_size("dp")
    total, width = cotangent.shape
    feats = queries.shape[1]
    mrows = keys.shape[0] * n_dp
    heads = feats // HDIM
    spans = total // SPAN
    cols = width // n_tensor
    keep = mrows // (n_section * n_tensor)
    turns = spans // n_section
    bf16, f32 = jnp.bfloat16, jnp.float32
    vmem = pl.BlockSpec(memory_space=pltpu.VMEM)
    anywhere = pl.BlockSpec(memory_space=pl.ANY)
    dma = pltpu.SemaphoreType.DMA
    return pl.pallas_call(
        functools.partial(chain_kernel, n_section, n_tensor, n_dp),
        out_shape=[
            jax.ShapeDtypeStruct((SPAN, width), bf16),
            jax.ShapeDtypeStruct((keep, width), bf16),
            jax.ShapeDtypeStruct((total, width), bf16),
            jax.ShapeDtypeStruct((total, feats), bf16),
            jax.ShapeDtypeStruct((total, feats), bf16),
            jax.ShapeDtypeStruct((mrows, feats), bf16),
            jax.ShapeDtypeStruct((mrows, feats), bf16),
        ],
        in_specs=[anywhere] + [vmem] * 3 + [anywhere, vmem, anywhere, anywhere],
        out_specs=[anywhere] * 7,
        scratch_shapes=[
            pltpu.VMEM((total, width), bf16),
            pltpu.VMEM((spans, SPAN + 2 * NTOK, feats), bf16),
            pltpu.VMEM((spans, SPAN, feats), bf16),
            pltpu.VMEM((spans, SPAN, feats), bf16),
            pltpu.VMEM((spans, SPAN, feats), bf16),
            pltpu.VMEM((spans, SPAN, feats), bf16),
            pltpu.VMEM((spans, n_tensor - 1, SPAN, cols), bf16),
            pltpu.VMEM((spans, SPAN, cols), f32),
            pltpu.VMEM((spans, n_tensor - 1, SPAN, cols), bf16),
            pltpu.VMEM((spans, SPAN, cols), bf16),
            pltpu.VMEM((SPAN, width), bf16),
            pltpu.VMEM((total, feats), bf16),
            pltpu.VMEM((total, feats), bf16),
            pltpu.VMEM((mrows, feats), bf16),
            pltpu.VMEM((mrows, feats), bf16),
            pltpu.VMEM((spans, heads, SPAN, NTOK), f32),
            pltpu.VMEM((spans, heads, SPAN, NTOK), bf16),
            pltpu.VMEM((spans, SPAN, feats), bf16),
            pltpu.VMEM((spans, heads, SPAN, NTOK), bf16),
            pltpu.VMEM((width, feats), bf16),
            pltpu.VMEM((width, feats), bf16),
            pltpu.VMEM((width, feats), bf16),
            pltpu.VMEM((spans, NTOK, width), bf16),
            pltpu.VMEM((n_section - 1, turns, NTOK, width), bf16),
            pltpu.VMEM((turns, NTOK // keep, keep, width), bf16),
            pltpu.VMEM((n_tensor - 1, keep, width), bf16),
            pltpu.VMEM((keep, width), bf16),
            dma((7,)),
            dma((spans,)),
            dma((spans,)),
            dma((spans,)),
            dma((spans,)),
            dma((spans,)),
            dma((spans,)),
            dma((spans,)),
            dma((spans,)),
            dma((spans,)),
            dma((spans,)),
            dma((spans,)),
            dma,
            dma((spans,)),
            dma((n_section - 1, turns)),
            dma,
            dma,
        ],
        compiler_params=pltpu.CompilerParams(
            collective_id=0, has_side_effects=True, vmem_limit_bytes=48 * 2**20
        ),
    )(cotangent, queries, keys, values, weight_query, weight_out, weight_key, weight_value)


def on_device(cotangent, queries, keys_values, streams_in, neighbours, w_query, w_key_value, w_out):
    weight_key = w_key_value[0][:, 0]
    weight_value = w_key_value[0][:, 1]
    streams, neighbour_part, grad, dq, attended, grad_k, grad_v = run_chain(
        cotangent,
        queries[0],
        keys_values[0][:, 0],
        keys_values[0][:, 1],
        w_query[0],
        w_out[0],
        weight_key,
        weight_value,
    )
    grad_query = contract_rows(streams_in[0], dq).astype(jnp.bfloat16)
    grad_key = contract_rows(neighbours, grad_k).astype(jnp.bfloat16)
    grad_value = contract_rows(neighbours, grad_v).astype(jnp.bfloat16)
    grad_pair = jnp.stack([grad_key, grad_value], axis=1)
    grad_out = contract_rows(attended, grad).astype(jnp.bfloat16)
    return (streams[None], neighbour_part, grad_query[None], grad_pair[None], grad_out[None])


def solution(mesh):
    in_specs = (
        P(None, "dp"),
        P("section", "dp", "tensor"),
        P("section", "dp", None, "tensor"),
        P("section", None, "dp"),
        P(None, "dp"),
        P("section", "dp", "tensor"),
        P("section", "dp", None, "tensor"),
        P("section", "tensor", "dp"),
    )
    out_specs = (
        P("section", "tensor", "dp"),
        P(("section", "tensor"), "dp"),
        P("section", "dp", "tensor"),
        P("section", "dp", None, "tensor"),
        P("section", "tensor", "dp"),
    )
    return jax.shard_map(
        on_device, mesh=mesh, in_specs=in_specs, out_specs=out_specs, check_vma=False
    )
```

```python
import functools

import jax
import jax.numpy as jnp
from jax import lax
from jax.experimental import pallas as pl
from jax.experimental.pallas import tpu as pltpu
from jax.sharding import PartitionSpec as P

HDIM = 128
SPAN = 64
NTOK = 128
SCALE = HDIM ** (-0.5)
MESH = pl.DeviceIdType.MESH


def contract_rows(left, right):
    return lax.dot_general(
        left, right, (((0,), (0,)), ((), ())), preferred_element_type=jnp.float32
    )


def contract_cols(left, right):
    return lax.dot_general(
        left, right, (((1,), (1,)), ((), ())), preferred_element_type=jnp.float32
    )


def wait_bytes(ref, sem):
    pltpu.make_async_copy(ref, ref, sem).wait()


def chain_kernel(
    n_section,
    n_tensor,
    n_dp,
    cot_ref,
    q_ref,
    kv_ref,
    wq_hbm,
    wo_ref,
    wkv_hbm,
    in_hbm,
    near_hbm,
    streams_out,
    near_out,
    query_out,
    pair_out,
    outer_out,
    g_ref,
    qkv,
    pair_part,
    pair_recv,
    z_part,
    z_recv,
    part,
    part_own,
    part_recv,
    new_ref,
    streams_ref,
    dq_ref,
    att_ref,
    dk_ref,
    dv_ref,
    probs,
    half,
    gatt,
    gscore,
    wq_ref,
    wkv_ref,
    in_ref,
    raw_ref,
    in_turned,
    raw_turned,
    query_ref,
    pair_ref,
    outer_ref,
    near_part,
    near_recv,
    sum_part,
    sum_recv,
    near_ref,
    copy_sem,
    qkv_send,
    qkv_sem,
    pair_send,
    pair_sem,
    z_send,
    z_sem,
    part_send,
    part_sem,
    g_send,
    g_sem,
    stream_send,
    stream_sem,
    near_send,
    near_sem,
    sum_send,
    sum_sem,
):
    sec = lax.axis_index("section")
    ten = lax.axis_index("tensor")
    dpp = lax.axis_index("dp")
    width = g_ref.shape[1]
    spans = g_ref.shape[0] // SPAN
    owned = spans // n_dp
    cols = width // n_tensor
    feats = q_ref.shape[1]
    heads = feats // HDIM
    mine = pl.ds(pl.multiple_of(ten * cols, cols), cols)
    sibling = dpp + 1 - 2 * lax.rem(dpp, 2)
    across = lax.rem(dpp + 2, n_dp)

    def dp_peer(r):
        return lax.rem(dpp + r, n_dp)

    def ten_peer(r):
        return lax.rem(ten + r, n_tensor)

    share_spans = spans // n_section
    weights = [
        pltpu.make_async_copy(wq_hbm, wq_ref, copy_sem.at[1]),
        pltpu.make_async_copy(wkv_hbm, wkv_ref, copy_sem.at[2]),
        pltpu.make_async_copy(in_hbm, in_ref, copy_sem.at[3]),
        pltpu.make_async_copy(near_hbm, raw_ref, copy_sem.at[4]),
    ]

    def span_at(t):
        return lax.rem(t + owned, spans)

    def token_rows(c):
        return pl.ds(pl.multiple_of(c * SPAN, SPAN), SPAN)

    def pair_rows(c):
        return pl.ds(pl.multiple_of(c * NTOK, NTOK), NTOK)

    def send(src, dst, send_sem, recv_sem, device):
        pltpu.make_async_remote_copy(
            src_ref=src,
            dst_ref=dst,
            send_sem=send_sem,
            recv_sem=recv_sem,
            device_id=device,
            device_id_type=MESH,
        ).start()

    barrier = pltpu.get_barrier_semaphore()
    for r in range(1, n_dp):
        pl.semaphore_signal(barrier, inc=1, device_id={"dp": dp_peer(r)}, device_id_type=MESH)
    for r in range(1, n_tensor):
        pl.semaphore_signal(barrier, inc=1, device_id={"tensor": ten_peer(r)}, device_id_type=MESH)

    for r in range(1, n_section):
        there = lax.rem(sec + r, n_section)
        pl.semaphore_signal(barrier, inc=1, device_id={"section": there}, device_id_type=MESH)

    @pl.when(sec > 0)
    def _():
        for r in range(n_tensor):
            pl.semaphore_signal(
                barrier, inc=1, device_id={"section": sec - 1, "tensor": ten_peer(r)}, device_id_type=MESH
            )

    @pl.when(sec < n_section - 1)
    def _():
        for r in range(n_tensor):
            pl.semaphore_signal(
                barrier, inc=1, device_id={"section": sec + 1, "tensor": ten_peer(r)}, device_id_type=MESH
            )

    @pl.when(sec == n_section - 1)
    def _():
        pltpu.make_async_copy(cot_ref, g_ref, copy_sem.at[0]).start()

    for weight in weights:
        weight.start()
    for i in range(owned):
        block = qkv.at[dpp * owned + i]
        block[0:SPAN, :] = q_ref[i * SPAN : (i + 1) * SPAN, :]
        block[SPAN : SPAN + NTOK, :] = kv_ref[0, i * NTOK : (i + 1) * NTOK, :]
        block[SPAN + NTOK : SPAN + 2 * NTOK, :] = kv_ref[1, i * NTOK : (i + 1) * NTOK, :]

    edge = jnp.where(sec > 0, n_tensor, 0) + jnp.where(sec < n_section - 1, n_tensor, 0)
    pl.semaphore_wait(barrier, n_dp - 1 + n_tensor - 1 + n_section - 1 + edge)

    @pl.when(sec == n_section - 1)
    def _():
        pltpu.make_async_copy(cot_ref, g_ref, copy_sem.at[0]).wait()

    key_rows = slice(SPAN, SPAN + NTOK)
    value_rows = slice(SPAN + NTOK, SPAN + 2 * NTOK)

    def head_lanes(h):
        return slice(h * HDIM, (h + 1) * HDIM)

    def share(t):
        c = span_at(t)

        @pl.when(c // owned == dpp)
        def _():
            send(qkv.at[c], qkv.at[c], qkv_send.at[c], qkv_sem.at[c], {"dp": across})
            send(qkv.at[c], qkv.at[c], qkv_send.at[c], qkv_sem.at[c], {"dp": sibling})

    def relay(t):
        c = span_at(t)

        @pl.when(c // owned == across)
        def _():
            wait_bytes(qkv.at[c], qkv_sem.at[c])
            send(qkv.at[c], qkv.at[c], qkv_send.at[c], qkv_sem.at[c], {"dp": sibling})

    def stage_a(t):
        c = span_at(t)

        @pl.when(sec < n_section - 1)
        def _():
            wait_bytes(g_ref.at[token_rows(c)], g_sem.at[c])

        out = contract_cols(g_ref[token_rows(c), :], wo_ref[...])
        pair_part[c] = out.astype(jnp.bfloat16)
        send(pair_part.at[c], pair_recv.at[c], pair_send.at[c], pair_sem.at[c], {"dp": sibling})

    def stage_a2(t):
        c = span_at(t)
        wait_bytes(pair_recv.at[c], pair_sem.at[c])
        total = pair_part[c].astype(jnp.float32) + pair_recv[c].astype(jnp.float32)
        z_part[c] = total.astype(jnp.bfloat16)
        send(z_part.at[c], z_recv.at[c], z_send.at[c], z_sem.at[c], {"dp": across})

    def stage_p(t):
        c = span_at(t)

        @pl.when(jnp.logical_and(c // owned != dpp, c // owned != across))
        def _():
            wait_bytes(qkv.at[c], qkv_sem.at[c])

        for h in range(heads):
            lanes = head_lanes(h)
            scores = contract_cols(qkv[c, 0:SPAN, lanes], qkv[c, key_rows, lanes]) * SCALE
            expo = jnp.exp(scores - jnp.max(scores, axis=-1, keepdims=True))
            prob = expo / jnp.sum(expo, axis=-1, keepdims=True)
            prob_half = prob.astype(jnp.bfloat16)
            probs[c, h] = prob
            half[c, h] = prob_half
            attended = jnp.dot(
                prob_half, qkv[c, value_rows, lanes], preferred_element_type=jnp.float32
            )
            att_ref[token_rows(c), lanes] = attended.astype(jnp.bfloat16)

    def stage_bc(t):
        c = span_at(t)
        wait_bytes(z_recv.at[c], z_sem.at[c])
        total = z_part[c].astype(jnp.float32) + z_recv[c].astype(jnp.float32)
        grad = total.astype(jnp.bfloat16)
        gatt[c] = grad
        for h in range(heads):
            lanes = head_lanes(h)
            grad_probs = contract_cols(grad[:, lanes], qkv[c, value_rows, lanes])
            prob = probs[c, h]
            delta = jnp.sum(prob * grad_probs, axis=-1, keepdims=True)
            grad_scores = (prob * (grad_probs - delta) * SCALE).astype(jnp.bfloat16)
            gscore[c, h] = grad_scores
            dq = jnp.dot(grad_scores, qkv[c, key_rows, lanes], preferred_element_type=jnp.float32)
            dq_ref[token_rows(c), lanes] = dq.astype(jnp.bfloat16)
        rows = dq_ref[token_rows(c), :]
        for r in list(range(1, n_tensor)) + [0]:
            peer = ten_peer(r)
            weight = wq_ref[pl.ds(pl.multiple_of(peer * cols, cols), cols), :]
            out = contract_cols(rows, weight)
            if r == 0:
                part_own[c] = out
            else:
                part[c, r - 1] = out.astype(jnp.bfloat16)
                send(
                    part.at[c, r - 1],
                    part_recv.at[c, r - 1],
                    part_send.at[c],
                    part_sem.at[c],
                    {"tensor": peer},
                )

    def stage_d(t):
        c = span_at(t)
        wait_bytes(part_recv.at[c], part_sem.at[c])
        total = g_ref[token_rows(c), mine].astype(jnp.float32) + part_own[c]
        for r in range(1, n_tensor):
            total = total + part_recv[c, r - 1].astype(jnp.float32)
        new_ref[c] = total.astype(jnp.bfloat16)

        @pl.when(sec > 0)
        def _():
            for r in range(n_tensor):
                send(
                    new_ref.at[c],
                    g_ref.at[token_rows(c), mine],
                    g_send.at[c],
                    g_sem.at[c],
                    {"section": sec - 1, "tensor": ten_peer(r)},
                )

        @pl.when(c != ten)
        def _():
            send(new_ref.at[c], streams_ref.at[:, mine], stream_send.at[c], stream_sem, {"tensor": c})

        @pl.when(c == ten)
        def _():
            streams_ref[:, mine] = new_ref[c]

    def stage_k(t):
        c = span_at(t)
        for h in range(heads):
            lanes = head_lanes(h)
            grad_k = contract_rows(gscore[c, h], qkv[c, 0:SPAN, lanes])
            dk_ref[pair_rows(c), lanes] = grad_k.astype(jnp.bfloat16)
            grad_v = contract_rows(half[c, h], gatt[c, :, lanes])
            dv_ref[pair_rows(c), lanes] = grad_v.astype(jnp.bfloat16)

    def stage_n(c):
        owner = c // share_spans
        for low in range(0, width, 512):
            block = slice(low, low + 512)
            out = contract_cols(dk_ref[pair_rows(c), :], wkv_ref[0, block, :])
            out = out + contract_cols(dv_ref[pair_rows(c), :], wkv_ref[1, block, :])
            near_part[c, :, block] = out.astype(jnp.bfloat16)

        @pl.when(owner != sec)
        def _():
            slot = lax.rem(sec - owner + n_section, n_section) - 1
            turn = lax.rem(c, share_spans)
            send(
                near_part.at[c],
                near_recv.at[slot, turn],
                near_send.at[c],
                near_sem.at[slot, turn],
                {"section": owner},
            )

    last = sec == n_section - 1

    def each(count, step):
        def body(i, carry):
            step(i)
            return carry

        lax.fori_loop(0, count, body, 0)

    block_cols = 256

    def turn_inputs(j):
        block = pl.ds(pl.multiple_of(j * block_cols, block_cols), block_cols)
        in_turned[block, :] = in_ref[:, block].T
        raw_turned[block, :] = raw_ref[:, block].T

    def weight_grads(j):
        block = pl.ds(pl.multiple_of(j * block_cols, block_cols), block_cols)
        grad_query = jnp.dot(in_turned[block, :], dq_ref[...], preferred_element_type=jnp.float32)
        query_ref[block, :] = grad_query.astype(jnp.bfloat16)
        grad_key = jnp.dot(raw_turned[block, :], dk_ref[...], preferred_element_type=jnp.float32)
        pair_ref[0, block, :] = grad_key.astype(jnp.bfloat16)
        grad_value = jnp.dot(raw_turned[block, :], dv_ref[...], preferred_element_type=jnp.float32)
        pair_ref[1, block, :] = grad_value.astype(jnp.bfloat16)
        grad_outer = contract_rows(att_ref[...], g_ref[:, block])
        outer_ref[:, block] = grad_outer.astype(jnp.bfloat16)

    blocks = width // block_cols

    @pl.when(jnp.logical_not(last))
    def _():
        each(spans, share)
        each(spans, relay)
        for weight in weights:
            weight.wait()
        each(spans, stage_p)
        each(blocks, turn_inputs)

    @pl.when(last)
    def _():
        share(0)

    def tick(t, carry):
        first = t < spans
        second = jnp.logical_and(t > 0, t <= spans)

        @pl.when(jnp.logical_and(last, jnp.logical_and(first, t > 0)))
        def _():
            relay(t)

        @pl.when(first)
        def _():
            stage_a(t)

        @pl.when(jnp.logical_and(last, jnp.logical_and(first, t > 0)))
        def _():
            stage_p(t)

        @pl.when(jnp.logical_and(sec == 0, t > 1))
        def _():
            stage_k(t - 2)

        @pl.when(first)
        def _():
            stage_a2(t)

        @pl.when(jnp.logical_and(last, t < spans - 1))
        def _():
            share(t + 1)

        @pl.when(jnp.logical_and(last, t == 0))
        def _():
            relay(0)
            stage_p(0)
            for weight in weights:
                weight.wait()

        @pl.when(jnp.logical_and(sec == 0, t > 1))
        def _():
            stage_n(span_at(t - 2))

        @pl.when(second)
        def _():
            stage_bc(t - 1)

        @pl.when(t > 1)
        def _():
            stage_d(t - 2)

        return carry

    lax.fori_loop(0, spans + 2, tick, 0)

    outs = [
        pltpu.make_async_copy(query_ref, query_out, copy_sem.at[0]),
        pltpu.make_async_copy(pair_ref, pair_out, copy_sem.at[1]),
        pltpu.make_async_copy(outer_ref, outer_out, copy_sem.at[2]),
        pltpu.make_async_copy(streams_ref, streams_out, copy_sem.at[5]),
    ]

    near_copy = pltpu.make_async_copy(near_ref, near_out, copy_sem.at[6])

    @pl.when(sec > 0)
    def _():
        each(spans, stage_k)
        each(spans, stage_n)

    @pl.when(last)
    def _():
        each(blocks, turn_inputs)

    @pl.when(sec > 0)
    def _():
        each(blocks, weight_grads)
        for out in outs[:-1]:
            out.start()

    keep = sum_part.shape[2]
    quarter = sum_part.shape[1]

    def sum_sections(turn, carry):
        c = sec * share_spans + turn
        for slot in range(n_section - 1):
            wait_bytes(near_recv.at[slot, turn], near_sem.at[slot, turn])
        for piece in range(quarter):
            rows = slice(piece * keep, (piece + 1) * keep)
            total = near_part[c, rows, :].astype(jnp.float32)
            for slot in range(n_section - 1):
                total = total + near_recv[slot, turn, rows, :].astype(jnp.float32)
            sum_part[turn, piece] = total.astype(jnp.bfloat16)
        for step in range(quarter):
            piece = lax.rem(ten + step, quarter)
            peer = turn * quarter + piece

            @pl.when(peer != ten)
            def _():
                send(
                    sum_part.at[turn, piece],
                    sum_recv.at[lax.rem(ten - peer + n_tensor, n_tensor) - 1],
                    sum_send,
                    sum_sem,
                    {"tensor": peer},
                )

        return carry

    lax.fori_loop(0, share_spans, sum_sections, 0)

    @pl.when(sec == 0)
    def _():
        each(blocks, weight_grads)
        for out in outs[:-1]:
            out.start()

    wait_bytes(part_recv.at[0], stream_sem)
    outs[-1].start()
    wait_bytes(sum_recv, sum_sem)
    total = sum_part[ten // quarter, lax.rem(ten, quarter)].astype(jnp.float32)
    for slot in range(n_tensor - 1):
        total = total + sum_recv[slot].astype(jnp.float32)
    near_ref[...] = total.astype(jnp.bfloat16)
    near_copy.start()

    def drain(c, carry):
        wait_bytes(pair_recv.at[c], pair_send.at[c])
        wait_bytes(z_recv.at[c], z_send.at[c])
        wait_bytes(part_recv.at[c], part_send.at[c])

        @pl.when(c // owned == dpp)
        def _():
            wait_bytes(qkv.at[pl.ds(0, 2)], qkv_send.at[c])

        @pl.when(c // owned == across)
        def _():
            wait_bytes(qkv.at[c], qkv_send.at[c])

        @pl.when(c // share_spans != sec)
        def _():
            wait_bytes(near_part.at[c], near_send.at[c])

        @pl.when(sec > 0)
        def _():
            wait_bytes(g_ref.at[token_rows(c)], g_send.at[c])

        @pl.when(c != ten)
        def _():
            wait_bytes(new_ref.at[c], stream_send.at[c])

        return carry

    lax.fori_loop(0, spans, drain, 0)
    wait_bytes(sum_recv, sum_send)
    for out in outs:
        out.wait()
    near_copy.wait()


def run_chain(cotangent, queries, pairs, weight_query, weight_out, weight_pair, streams_in, neighbours):
    n_section = lax.axis_size("section")
    n_tensor = lax.axis_size("tensor")
    n_dp = lax.axis_size("dp")
    total, width = cotangent.shape
    feats = queries.shape[1]
    mrows = neighbours.shape[0]
    heads = feats // HDIM
    spans = total // SPAN
    cols = width // n_tensor
    keep = mrows // (n_section * n_tensor)
    turns = spans // n_section
    bf16, f32 = jnp.bfloat16, jnp.float32
    vmem = pl.BlockSpec(memory_space=pltpu.VMEM)
    anywhere = pl.BlockSpec(memory_space=pl.ANY)
    dma = pltpu.SemaphoreType.DMA
    return pl.pallas_call(
        functools.partial(chain_kernel, n_section, n_tensor, n_dp),
        out_shape=[
            jax.ShapeDtypeStruct((SPAN, width), bf16),
            jax.ShapeDtypeStruct((keep, width), bf16),
            jax.ShapeDtypeStruct((width, feats), bf16),
            jax.ShapeDtypeStruct((2, width, feats), bf16),
            jax.ShapeDtypeStruct((feats, width), bf16),
        ],
        in_specs=[anywhere, vmem, vmem, anywhere, vmem, anywhere, anywhere, anywhere],
        out_specs=[anywhere] * 5,
        scratch_shapes=[
            pltpu.VMEM((total, width), bf16),
            pltpu.VMEM((spans, SPAN + 2 * NTOK, feats), bf16),
            pltpu.VMEM((spans, SPAN, feats), bf16),
            pltpu.VMEM((spans, SPAN, feats), bf16),
            pltpu.VMEM((spans, SPAN, feats), bf16),
            pltpu.VMEM((spans, SPAN, feats), bf16),
            pltpu.VMEM((spans, n_tensor - 1, SPAN, cols), bf16),
            pltpu.VMEM((spans, SPAN, cols), f32),
            pltpu.VMEM((spans, n_tensor - 1, SPAN, cols), bf16),
            pltpu.VMEM((spans, SPAN, cols), bf16),
            pltpu.VMEM((SPAN, width), bf16),
            pltpu.VMEM((total, feats), bf16),
            pltpu.VMEM((total, feats), bf16),
            pltpu.VMEM((mrows, feats), bf16),
            pltpu.VMEM((mrows, feats), bf16),
            pltpu.VMEM((spans, heads, SPAN, NTOK), f32),
            pltpu.VMEM((spans, heads, SPAN, NTOK), bf16),
            pltpu.VMEM((spans, SPAN, feats), bf16),
            pltpu.VMEM((spans, heads, SPAN, NTOK), bf16),
            pltpu.VMEM((width, feats), bf16),
            pltpu.VMEM((2, width, feats), bf16),
            pltpu.VMEM((total, width), bf16),
            pltpu.VMEM((mrows, width), bf16),
            pltpu.VMEM((width, total), bf16),
            pltpu.VMEM((width, mrows), bf16),
            pltpu.VMEM((width, feats), bf16),
            pltpu.VMEM((2, width, feats), bf16),
            pltpu.VMEM((feats, width), bf16),
            pltpu.VMEM((spans, NTOK, width), bf16),
            pltpu.VMEM((n_section - 1, turns, NTOK, width), bf16),
            pltpu.VMEM((turns, NTOK // keep, keep, width), bf16),
            pltpu.VMEM((n_tensor - 1, keep, width), bf16),
            pltpu.VMEM((keep, width), bf16),
            dma((7,)),
            dma((spans,)),
            dma((spans,)),
            dma((spans,)),
            dma((spans,)),
            dma((spans,)),
            dma((spans,)),
            dma((spans,)),
            dma((spans,)),
            dma((spans,)),
            dma((spans,)),
            dma((spans,)),
            dma,
            dma((spans,)),
            dma((n_section - 1, turns)),
            dma,
            dma,
        ],
        compiler_params=pltpu.CompilerParams(
            collective_id=0, has_side_effects=True, vmem_limit_bytes=60 * 2**20
        ),
    )(cotangent, queries, pairs, weight_query, weight_out, weight_pair, streams_in, neighbours)


def on_device(cotangent, queries, keys_values, streams_in, neighbours, w_query, w_key_value, w_out):
    streams, neighbour_part, grad_query, grad_pair, grad_out = run_chain(
        cotangent,
        queries[0],
        jnp.swapaxes(keys_values[0], 0, 1),
        w_query[0],
        w_out[0],
        jnp.swapaxes(w_key_value[0], 0, 1),
        streams_in[0],
        neighbours,
    )
    grad_pair = jnp.swapaxes(grad_pair, 0, 1)
    return (streams[None], neighbour_part, grad_query[None], grad_pair[None], grad_out[None])


def solution(mesh):
    in_specs = (
        P(None, "dp"),
        P("section", "dp", "tensor"),
        P("section", "dp", None, "tensor"),
        P("section", None, "dp"),
        P(None, "dp"),
        P("section", "dp", "tensor"),
        P("section", "dp", None, "tensor"),
        P("section", "tensor", "dp"),
    )
    out_specs = (
        P("section", "tensor", "dp"),
        P(("section", "tensor"), "dp"),
        P("section", "dp", "tensor"),
        P("section", "dp", None, "tensor"),
        P("section", "tensor", "dp"),
    )
    return jax.shard_map(
        on_device, mesh=mesh, in_specs=in_specs, out_specs=out_specs, check_vma=False
    )
```

```python
import functools

import jax
import jax.numpy as jnp
from jax import lax
from jax.experimental import pallas as pl
from jax.experimental.pallas import tpu as pltpu
from jax.sharding import PartitionSpec as P

HDIM = 128
SPAN = 64
NTOK = 128
SCALE = HDIM ** (-0.5)
MESH = pl.DeviceIdType.MESH


def contract_rows(left, right):
    return lax.dot_general(
        left, right, (((0,), (0,)), ((), ())), preferred_element_type=jnp.float32
    )


def contract_cols(left, right):
    return lax.dot_general(
        left, right, (((1,), (1,)), ((), ())), preferred_element_type=jnp.float32
    )


def wait_bytes(ref, sem):
    pltpu.make_async_copy(ref, ref, sem).wait()


def chain_kernel(
    n_section,
    n_tensor,
    n_dp,
    cot_ref,
    q_ref,
    kv_ref,
    wq_hbm,
    wo_ref,
    wkv_hbm,
    in_hbm,
    near_hbm,
    streams_out,
    near_out,
    query_out,
    pair_out,
    outer_out,
    g_ref,
    qkv,
    pair_part,
    pair_recv,
    z_part,
    z_recv,
    part,
    part_own,
    part_recv,
    new_ref,
    streams_ref,
    dq_ref,
    att_ref,
    dk_ref,
    dv_ref,
    probs,
    half,
    gatt,
    gscore,
    wq_ref,
    wkv_ref,
    in_ref,
    raw_ref,
    in_turned,
    raw_turned,
    query_ref,
    pair_ref,
    outer_ref,
    near_part,
    front_recv,
    plane_recv,
    plane_sum,
    far_recv,
    sum_recv,
    near_ref,
    copy_sem,
    qkv_send,
    qkv_sem,
    pair_send,
    pair_sem,
    z_send,
    z_sem,
    part_send,
    part_sem,
    g_send,
    g_sem,
    stream_send,
    stream_sem,
    near_send,
    front_sem,
    plane_sem,
    far_send,
    far_sem,
    sum_send,
    sum_sem,
):
    sec = lax.axis_index("section")
    ten = lax.axis_index("tensor")
    dpp = lax.axis_index("dp")
    width = g_ref.shape[1]
    spans = g_ref.shape[0] // SPAN
    owned = spans // n_dp
    cols = width // n_tensor
    feats = q_ref.shape[1]
    heads = feats // HDIM
    mine = pl.ds(pl.multiple_of(ten * cols, cols), cols)
    sibling = dpp + 1 - 2 * lax.rem(dpp, 2)
    across = lax.rem(dpp + 2, n_dp)

    def dp_peer(r):
        return lax.rem(dpp + r, n_dp)

    def ten_peer(r):
        return lax.rem(ten + r, n_tensor)

    share_spans = spans // n_section
    weights = [
        pltpu.make_async_copy(wq_hbm, wq_ref, copy_sem.at[1]),
        pltpu.make_async_copy(wkv_hbm, pair_ref, copy_sem.at[2]),
        pltpu.make_async_copy(in_hbm, in_ref, copy_sem.at[3]),
        pltpu.make_async_copy(near_hbm, raw_ref, copy_sem.at[4]),
    ]

    def span_at(t):
        return lax.rem(t + owned, spans)

    def token_rows(c):
        return pl.ds(pl.multiple_of(c * SPAN, SPAN), SPAN)

    def pair_rows(c):
        return pl.ds(pl.multiple_of(c * NTOK, NTOK), NTOK)

    def send(src, dst, send_sem, recv_sem, device):
        pltpu.make_async_remote_copy(
            src_ref=src,
            dst_ref=dst,
            send_sem=send_sem,
            recv_sem=recv_sem,
            device_id=device,
            device_id_type=MESH,
        ).start()

    barrier = pltpu.get_barrier_semaphore()
    for r in range(1, n_dp):
        pl.semaphore_signal(barrier, inc=1, device_id={"dp": dp_peer(r)}, device_id_type=MESH)
    for step in range(n_section):
        for r in range(n_tensor):
            if step or r:
                there = {"section": lax.rem(sec + step, n_section), "tensor": ten_peer(r)}
                pl.semaphore_signal(barrier, inc=1, device_id=there, device_id_type=MESH)

    @pl.when(sec == n_section - 1)
    def _():
        pltpu.make_async_copy(cot_ref, g_ref, copy_sem.at[0]).start()

    for weight in weights:
        weight.start()
    for i in range(owned):
        block = qkv.at[dpp * owned + i]
        block[0:SPAN, :] = q_ref[i * SPAN : (i + 1) * SPAN, :]
        block[SPAN : SPAN + NTOK, :] = kv_ref[0, i * NTOK : (i + 1) * NTOK, :]
        block[SPAN + NTOK : SPAN + 2 * NTOK, :] = kv_ref[1, i * NTOK : (i + 1) * NTOK, :]

    pl.semaphore_wait(barrier, n_dp - 1 + n_section * n_tensor - 1)

    @pl.when(sec == n_section - 1)
    def _():
        pltpu.make_async_copy(cot_ref, g_ref, copy_sem.at[0]).wait()

    key_rows = slice(SPAN, SPAN + NTOK)
    value_rows = slice(SPAN + NTOK, SPAN + 2 * NTOK)

    def head_lanes(h):
        return slice(h * HDIM, (h + 1) * HDIM)

    def share(t):
        c = span_at(t)

        @pl.when(c // owned == dpp)
        def _():
            send(qkv.at[c], qkv.at[c], qkv_send.at[c], qkv_sem.at[c], {"dp": across})
            send(qkv.at[c], qkv.at[c], qkv_send.at[c], qkv_sem.at[c], {"dp": sibling})

    def relay(t):
        c = span_at(t)

        @pl.when(c // owned == across)
        def _():
            wait_bytes(qkv.at[c], qkv_sem.at[c])
            send(qkv.at[c], qkv.at[c], qkv_send.at[c], qkv_sem.at[c], {"dp": sibling})

    def stage_a(t):
        c = span_at(t)

        @pl.when(sec < n_section - 1)
        def _():
            wait_bytes(g_ref.at[token_rows(c)], g_sem.at[c])

        out = contract_cols(g_ref[token_rows(c), :], wo_ref[...])
        pair_part[c] = out.astype(jnp.bfloat16)
        send(pair_part.at[c], pair_recv.at[c], pair_send.at[c], pair_sem.at[c], {"dp": sibling})

    def stage_a2(t):
        c = span_at(t)
        wait_bytes(pair_recv.at[c], pair_sem.at[c])
        total = pair_part[c].astype(jnp.float32) + pair_recv[c].astype(jnp.float32)
        z_part[c] = total.astype(jnp.bfloat16)
        send(z_part.at[c], z_recv.at[c], z_send.at[c], z_sem.at[c], {"dp": across})

    def stage_p(t):
        c = span_at(t)

        @pl.when(jnp.logical_and(c // owned != dpp, c // owned != across))
        def _():
            wait_bytes(qkv.at[c], qkv_sem.at[c])

        for h in range(heads):
            lanes = head_lanes(h)
            scores = contract_cols(qkv[c, 0:SPAN, lanes], qkv[c, key_rows, lanes]) * SCALE
            expo = jnp.exp(scores - jnp.max(scores, axis=-1, keepdims=True))
            prob = expo / jnp.sum(expo, axis=-1, keepdims=True)
            prob_half = prob.astype(jnp.bfloat16)
            probs[c, h] = prob
            half[c, h] = prob_half
            attended = jnp.dot(
                prob_half, qkv[c, value_rows, lanes], preferred_element_type=jnp.float32
            )
            att_ref[token_rows(c), lanes] = attended.astype(jnp.bfloat16)

    def stage_bc(t):
        c = span_at(t)
        wait_bytes(z_recv.at[c], z_sem.at[c])
        total = z_part[c].astype(jnp.float32) + z_recv[c].astype(jnp.float32)
        grad = total.astype(jnp.bfloat16)
        gatt[c] = grad
        for h in range(heads):
            lanes = head_lanes(h)
            grad_probs = contract_cols(grad[:, lanes], qkv[c, value_rows, lanes])
            prob = probs[c, h]
            delta = jnp.sum(prob * grad_probs, axis=-1, keepdims=True)
            grad_scores = (prob * (grad_probs - delta) * SCALE).astype(jnp.bfloat16)
            gscore[c, h] = grad_scores
            dq = jnp.dot(grad_scores, qkv[c, key_rows, lanes], preferred_element_type=jnp.float32)
            dq_ref[token_rows(c), lanes] = dq.astype(jnp.bfloat16)
        rows = dq_ref[token_rows(c), :]
        for r in list(range(1, n_tensor)) + [0]:
            peer = ten_peer(r)
            weight = wq_ref[pl.ds(pl.multiple_of(peer * cols, cols), cols), :]
            out = contract_cols(rows, weight)
            if r == 0:
                part_own[c] = out
            else:
                part[c, r - 1] = out.astype(jnp.bfloat16)
                send(
                    part.at[c, r - 1],
                    part_recv.at[c, r - 1],
                    part_send.at[c],
                    part_sem.at[c],
                    {"tensor": peer},
                )

    def stage_d(t):
        c = span_at(t)
        wait_bytes(part_recv.at[c], part_sem.at[c])
        total = g_ref[token_rows(c), mine].astype(jnp.float32) + part_own[c]
        for r in range(1, n_tensor):
            total = total + part_recv[c, r - 1].astype(jnp.float32)
        new_ref[c] = total.astype(jnp.bfloat16)

        @pl.when(sec > 0)
        def _():
            for r in range(n_tensor):
                send(
                    new_ref.at[c],
                    g_ref.at[token_rows(c), mine],
                    g_send.at[c],
                    g_sem.at[c],
                    {"section": sec - 1, "tensor": ten_peer(r)},
                )

        @pl.when(c != ten)
        def _():
            send(new_ref.at[c], streams_ref.at[:, mine], stream_send.at[c], stream_sem, {"tensor": c})

        @pl.when(c == ten)
        def _():
            streams_ref[:, mine] = new_ref[c]

    def stage_k(t):
        c = span_at(t)
        for h in range(heads):
            lanes = head_lanes(h)
            grad_k = contract_rows(gscore[c, h], qkv[c, 0:SPAN, lanes])
            dk_ref[pair_rows(c), lanes] = grad_k.astype(jnp.bfloat16)
            grad_v = contract_rows(half[c, h], gatt[c, :, lanes])
            dv_ref[pair_rows(c), lanes] = grad_v.astype(jnp.bfloat16)

    def stage_n(c):
        owner = c // share_spans
        for low in range(0, width, 512):
            block = slice(low, low + 512)
            out = contract_cols(dk_ref[pair_rows(c), :], wkv_ref[0, block, :])
            out = out + contract_cols(dv_ref[pair_rows(c), :], wkv_ref[1, block, :])
            near_part[c, :, block] = out.astype(jnp.bfloat16)

        turn = lax.rem(c, share_spans)

        @pl.when(jnp.logical_and(sec == 0, owner > 0))
        def _():
            send(
                near_part.at[c],
                front_recv.at[turn],
                near_send.at[c],
                front_sem.at[turn],
                {"section": owner},
            )

        @pl.when(jnp.logical_and(sec == 0, owner == 0))
        def _():
            front_recv[turn] = near_part[c]

        @pl.when(jnp.logical_and(sec > 0, c != ten))
        def _():
            send(
                near_part.at[c],
                plane_recv.at[lax.rem(ten - c + n_tensor, n_tensor) - 1],
                near_send.at[c],
                plane_sem,
                {"tensor": c},
            )

    last = sec == n_section - 1

    def each(count, step):
        def body(i, carry):
            step(i)
            return carry

        lax.fori_loop(0, count, body, 0)

    block_cols = 256

    def turn_inputs(j):
        block = pl.ds(pl.multiple_of(j * block_cols, block_cols), block_cols)
        in_turned[block, :] = in_ref[:, block].T
        raw_turned[block, :] = raw_ref[:, block].T
        wkv_ref[0, block, :] = pair_ref[block, 0, :]
        wkv_ref[1, block, :] = pair_ref[block, 1, :]

    def weight_grads(j):
        block = pl.ds(pl.multiple_of(j * block_cols, block_cols), block_cols)
        grad_query = jnp.dot(in_turned[block, :], dq_ref[...], preferred_element_type=jnp.float32)
        query_ref[block, :] = grad_query.astype(jnp.bfloat16)
        grad_key = jnp.dot(raw_turned[block, :], dk_ref[...], preferred_element_type=jnp.float32)
        pair_ref[block, 0, :] = grad_key.astype(jnp.bfloat16)
        grad_value = jnp.dot(raw_turned[block, :], dv_ref[...], preferred_element_type=jnp.float32)
        pair_ref[block, 1, :] = grad_value.astype(jnp.bfloat16)
        grad_outer = contract_rows(att_ref[...], g_ref[:, block])
        outer_ref[:, block] = grad_outer.astype(jnp.bfloat16)

    blocks = width // block_cols

    @pl.when(jnp.logical_not(last))
    def _():
        each(spans, share)
        each(spans, relay)
        for weight in weights:
            weight.wait()
        each(spans, stage_p)
        each(blocks, turn_inputs)

    @pl.when(last)
    def _():
        share(0)

    def tick(t, carry):
        first = t < spans
        second = jnp.logical_and(t > 0, t <= spans)

        @pl.when(first)
        def _():
            stage_a(t)

        @pl.when(jnp.logical_and(last, jnp.logical_and(first, t > 0)))
        def _():
            stage_p(t)

        @pl.when(jnp.logical_and(sec == 0, t > 1))
        def _():
            stage_k(t - 2)

        @pl.when(first)
        def _():
            stage_a2(t)

        @pl.when(jnp.logical_and(last, t < 3))
        def _():
            @pl.when(t == 0)
            def _():
                share(1)

            share(2 * t + 2)
            share(2 * t + 3)

        @pl.when(jnp.logical_and(last, t == 0))
        def _():
            relay(0)
            stage_p(0)
            for weight in weights:
                weight.wait()

        @pl.when(jnp.logical_and(last, t < spans - 1))
        def _():
            relay(t + 1)

        @pl.when(jnp.logical_and(sec == 0, t > 1))
        def _():
            stage_n(span_at(t - 2))

        @pl.when(second)
        def _():
            stage_bc(t - 1)

        @pl.when(t > 1)
        def _():
            stage_d(t - 2)

        return carry

    lax.fori_loop(0, spans + 2, tick, 0)

    outs = [
        pltpu.make_async_copy(query_ref, query_out, copy_sem.at[0]),
        pltpu.make_async_copy(pair_ref, pair_out, copy_sem.at[1]),
        pltpu.make_async_copy(outer_ref, outer_out, copy_sem.at[2]),
        pltpu.make_async_copy(streams_ref, streams_out, copy_sem.at[5]),
    ]

    near_copy = pltpu.make_async_copy(near_ref, near_out, copy_sem.at[6])

    @pl.when(sec > 0)
    def _():
        each(spans, stage_k)

    @pl.when(last)
    def _():
        each(blocks, turn_inputs)

    @pl.when(sec > 0)
    def _():
        each(spans, stage_n)
        each(blocks, weight_grads)
        for out in outs[:-1]:
            out.start()

    keep, quarter = near_ref.shape[0], NTOK // near_ref.shape[0]
    home = ten // share_spans
    first_peer = lax.rem(ten, share_spans) * quarter

    @pl.when(sec > 0)
    def _():
        wait_bytes(plane_recv, plane_sem)
        for piece in range(quarter):
            rows = slice(piece * keep, (piece + 1) * keep)
            total = near_part[ten, rows, :].astype(jnp.float32)
            for slot in range(n_tensor - 1):
                total = total + plane_recv[slot, rows, :].astype(jnp.float32)
            plane_sum[piece] = total.astype(jnp.bfloat16)
            here = jnp.logical_and(home == sec, first_peer + piece == ten)

            @pl.when(here)
            def _():
                far_recv[sec - 1] = plane_sum[piece]

            @pl.when(jnp.logical_not(here))
            def _():
                send(
                    plane_sum.at[piece],
                    far_recv.at[sec - 1],
                    far_send.at[piece],
                    far_sem.at[sec - 1],
                    {"section": home, "tensor": first_peer + piece},
                )

    def spread(turn):
        @pl.when(sec > 0)
        def _():
            wait_bytes(front_recv.at[turn], front_sem.at[turn])

        for step in range(quarter):
            piece = lax.rem(ten + step, quarter)
            peer = turn * quarter + piece

            @pl.when(peer != ten)
            def _():
                send(
                    front_recv.at[turn, pl.ds(pl.multiple_of(piece * keep, keep), keep)],
                    sum_recv.at[lax.rem(ten - peer + n_tensor, n_tensor) - 1],
                    sum_send,
                    sum_sem,
                    {"tensor": peer},
                )

    each(share_spans, spread)

    @pl.when(sec == 0)
    def _():
        each(blocks, weight_grads)
        for out in outs[:-1]:
            out.start()

    wait_bytes(part_recv.at[0], stream_sem)
    outs[-1].start()
    source = sec * share_spans + ten // quarter
    for slot in range(n_section - 1):

        @pl.when(jnp.logical_not(jnp.logical_and(sec == slot + 1, source == ten)))
        def _():
            wait_bytes(far_recv.at[slot], far_sem.at[slot])

    wait_bytes(sum_recv, sum_sem)
    own = pl.ds(pl.multiple_of(lax.rem(ten, quarter) * keep, keep), keep)
    total = front_recv[ten // quarter, own, :].astype(jnp.float32)
    for slot in range(n_tensor - 1):
        total = total + sum_recv[slot].astype(jnp.float32)
    for slot in range(n_section - 1):
        total = total + far_recv[slot].astype(jnp.float32)
    near_ref[...] = total.astype(jnp.bfloat16)
    near_copy.start()

    def drain(c, carry):
        wait_bytes(pair_recv.at[c], pair_send.at[c])
        wait_bytes(z_recv.at[c], z_send.at[c])
        wait_bytes(part_recv.at[c], part_send.at[c])

        @pl.when(c // owned == dpp)
        def _():
            wait_bytes(qkv.at[pl.ds(0, 2)], qkv_send.at[c])

        @pl.when(c // owned == across)
        def _():
            wait_bytes(qkv.at[c], qkv_send.at[c])

        @pl.when(jnp.logical_or(jnp.logical_and(sec == 0, c >= share_spans), jnp.logical_and(sec > 0, c != ten)))
        def _():
            wait_bytes(near_part.at[c], near_send.at[c])

        @pl.when(sec > 0)
        def _():
            wait_bytes(g_ref.at[token_rows(c)], g_send.at[c])

        @pl.when(c != ten)
        def _():
            wait_bytes(new_ref.at[c], stream_send.at[c])

        return carry

    lax.fori_loop(0, spans, drain, 0)
    wait_bytes(sum_recv, sum_send)
    for piece in range(quarter):

        @pl.when(jnp.logical_and(sec > 0, jnp.logical_not(jnp.logical_and(home == sec, first_peer + piece == ten))))
        def _():
            wait_bytes(plane_sum.at[piece], far_send.at[piece])

    for out in outs:
        out.wait()
    near_copy.wait()


def run_chain(cotangent, queries, pairs, weight_query, weight_out, weight_pair, streams_in, neighbours):
    n_section = lax.axis_size("section")
    n_tensor = lax.axis_size("tensor")
    n_dp = lax.axis_size("dp")
    total, width = cotangent.shape
    feats = queries.shape[1]
    mrows = neighbours.shape[0]
    heads = feats // HDIM
    spans = total // SPAN
    cols = width // n_tensor
    keep = mrows // (n_section * n_tensor)
    turns = spans // n_section
    bf16, f32 = jnp.bfloat16, jnp.float32
    vmem = pl.BlockSpec(memory_space=pltpu.VMEM)
    anywhere = pl.BlockSpec(memory_space=pl.ANY)
    dma = pltpu.SemaphoreType.DMA
    return pl.pallas_call(
        functools.partial(chain_kernel, n_section, n_tensor, n_dp),
        out_shape=[
            jax.ShapeDtypeStruct((SPAN, width), bf16),
            jax.ShapeDtypeStruct((keep, width), bf16),
            jax.ShapeDtypeStruct((width, feats), bf16),
            jax.ShapeDtypeStruct((width, 2, feats), bf16),
            jax.ShapeDtypeStruct((feats, width), bf16),
        ],
        in_specs=[anywhere, vmem, vmem, anywhere, vmem, anywhere, anywhere, anywhere],
        out_specs=[anywhere] * 5,
        scratch_shapes=[
            pltpu.VMEM((total, width), bf16),
            pltpu.VMEM((spans, SPAN + 2 * NTOK, feats), bf16),
            pltpu.VMEM((spans, SPAN, feats), bf16),
            pltpu.VMEM((spans, SPAN, feats), bf16),
            pltpu.VMEM((spans, SPAN, feats), bf16),
            pltpu.VMEM((spans, SPAN, feats), bf16),
            pltpu.VMEM((spans, n_tensor - 1, SPAN, cols), bf16),
            pltpu.VMEM((spans, SPAN, cols), f32),
            pltpu.VMEM((spans, n_tensor - 1, SPAN, cols), bf16),
            pltpu.VMEM((spans, SPAN, cols), bf16),
            pltpu.VMEM((SPAN, width), bf16),
            pltpu.VMEM((total, feats), bf16),
            pltpu.VMEM((total, feats), bf16),
            pltpu.VMEM((mrows, feats), bf16),
            pltpu.VMEM((mrows, feats), bf16),
            pltpu.VMEM((spans, heads, SPAN, NTOK), f32),
            pltpu.VMEM((spans, heads, SPAN, NTOK), bf16),
            pltpu.VMEM((spans, SPAN, feats), bf16),
            pltpu.VMEM((spans, heads, SPAN, NTOK), bf16),
            pltpu.VMEM((width, feats), bf16),
            pltpu.VMEM((2, width, feats), bf16),
            pltpu.VMEM((total, width), bf16),
            pltpu.VMEM((mrows, width), bf16),
            pltpu.VMEM((width, total), bf16),
            pltpu.VMEM((width, mrows), bf16),
            pltpu.VMEM((width, feats), bf16),
            pltpu.VMEM((width, 2, feats), bf16),
            pltpu.VMEM((feats, width), bf16),
            pltpu.VMEM((spans, NTOK, width), bf16),
            pltpu.VMEM((turns, NTOK, width), bf16),
            pltpu.VMEM((n_tensor - 1, NTOK, width), bf16),
            pltpu.VMEM((NTOK // keep, keep, width), bf16),
            pltpu.VMEM((n_section - 1, keep, width), bf16),
            pltpu.VMEM((n_tensor - 1, keep, width), bf16),
            pltpu.VMEM((keep, width), bf16),
            dma((7,)),
            dma((spans,)),
            dma((spans,)),
            dma((spans,)),
            dma((spans,)),
            dma((spans,)),
            dma((spans,)),
            dma((spans,)),
            dma((spans,)),
            dma((spans,)),
            dma((spans,)),
            dma((spans,)),
            dma,
            dma((spans,)),
            dma((turns,)),
            dma,
            dma((NTOK // keep,)),
            dma((n_section - 1,)),
            dma,
            dma,
        ],
        compiler_params=pltpu.CompilerParams(
            collective_id=0, has_side_effects=True, vmem_limit_bytes=60 * 2**20
        ),
    )(cotangent, queries, pairs, weight_query, weight_out, weight_pair, streams_in, neighbours)


def on_device(cotangent, queries, keys_values, streams_in, neighbours, w_query, w_key_value, w_out):
    streams, neighbour_part, grad_query, grad_pair, grad_out = run_chain(
        cotangent,
        queries[0],
        jnp.swapaxes(keys_values[0], 0, 1),
        w_query[0],
        w_out[0],
        w_key_value[0],
        streams_in[0],
        neighbours,
    )
    return (streams[None], neighbour_part, grad_query[None], grad_pair[None], grad_out[None])


def solution(mesh):
    in_specs = (
        P(None, "dp"),
        P("section", "dp", "tensor"),
        P("section", "dp", None, "tensor"),
        P("section", None, "dp"),
        P(None, "dp"),
        P("section", "dp", "tensor"),
        P("section", "dp", None, "tensor"),
        P("section", "tensor", "dp"),
    )
    out_specs = (
        P("section", "tensor", "dp"),
        P(("section", "tensor"), "dp"),
        P("section", "dp", "tensor"),
        P("section", "dp", None, "tensor"),
        P("section", "tensor", "dp"),
    )
    return jax.shard_map(
        on_device, mesh=mesh, in_specs=in_specs, out_specs=out_specs, check_vma=False
    )
```

```python
import functools

import jax
import jax.numpy as jnp
from jax import lax
from jax.experimental import pallas as pl
from jax.experimental.pallas import tpu as pltpu
from jax.sharding import PartitionSpec as P

HDIM = 128
SPAN = 64
NTOK = 128
SCALE = HDIM ** (-0.5)
MESH = pl.DeviceIdType.MESH


def contract_rows(left, right):
    return lax.dot_general(
        left, right, (((0,), (0,)), ((), ())), preferred_element_type=jnp.float32
    )


def contract_cols(left, right):
    return lax.dot_general(
        left, right, (((1,), (1,)), ((), ())), preferred_element_type=jnp.float32
    )


def wait_bytes(ref, sem):
    pltpu.make_async_copy(ref, ref, sem).wait()


def chain_kernel(
    n_section,
    n_tensor,
    n_dp,
    cot_ref,
    q_ref,
    kv_ref,
    wq_hbm,
    wo_ref,
    wkv_hbm,
    in_hbm,
    near_hbm,
    streams_out,
    near_out,
    query_out,
    pair_out,
    outer_out,
    g_ref,
    qkv,
    pair_part,
    pair_recv,
    z_part,
    z_recv,
    part,
    part_own,
    part_recv,
    new_ref,
    streams_ref,
    dq_ref,
    att_ref,
    dk_ref,
    dv_ref,
    probs,
    half,
    gatt,
    gscore,
    wq_ref,
    wkv_ref,
    in_ref,
    raw_ref,
    in_turned,
    raw_turned,
    query_ref,
    pair_ref,
    outer_ref,
    near_part,
    front_recv,
    plane_recv,
    plane_sum,
    far_recv,
    sum_recv,
    near_ref,
    copy_sem,
    qkv_send,
    qkv_sem,
    pair_send,
    pair_sem,
    z_send,
    z_sem,
    part_send,
    part_sem,
    g_send,
    g_sem,
    stream_send,
    stream_sem,
    near_send,
    front_sem,
    plane_sem,
    far_send,
    far_sem,
    sum_send,
    sum_sem,
):
    sec = lax.axis_index("section")
    ten = lax.axis_index("tensor")
    dpp = lax.axis_index("dp")
    width = g_ref.shape[1]
    spans = g_ref.shape[0] // SPAN
    owned = spans // n_dp
    cols = width // n_tensor
    feats = q_ref.shape[1]
    heads = feats // HDIM
    mine = pl.ds(pl.multiple_of(ten * cols, cols), cols)
    sibling = dpp + 1 - 2 * lax.rem(dpp, 2)
    across = lax.rem(dpp + 2, n_dp)

    def dp_peer(r):
        return lax.rem(dpp + r, n_dp)

    def ten_peer(r):
        return lax.rem(ten + r, n_tensor)

    share_spans = spans // n_section
    weights = [
        pltpu.make_async_copy(wq_hbm, wq_ref, copy_sem.at[1]),
        pltpu.make_async_copy(wkv_hbm, pair_ref, copy_sem.at[2]),
        pltpu.make_async_copy(in_hbm, in_ref, copy_sem.at[3]),
        pltpu.make_async_copy(near_hbm, raw_ref, copy_sem.at[4]),
    ]

    def span_at(t):
        return lax.rem(t + owned, spans)

    def token_rows(c):
        return pl.ds(pl.multiple_of(c * SPAN, SPAN), SPAN)

    def pair_rows(c):
        return pl.ds(pl.multiple_of(c * NTOK, NTOK), NTOK)

    def send(src, dst, send_sem, recv_sem, device):
        pltpu.make_async_remote_copy(
            src_ref=src,
            dst_ref=dst,
            send_sem=send_sem,
            recv_sem=recv_sem,
            device_id=device,
            device_id_type=MESH,
        ).start()

    barrier = pltpu.get_barrier_semaphore()
    for r in range(1, n_dp):
        pl.semaphore_signal(barrier, inc=1, device_id={"dp": dp_peer(r)}, device_id_type=MESH)
    for step in range(n_section):
        for r in range(n_tensor):
            if step or r:
                there = {"section": lax.rem(sec + step, n_section), "tensor": ten_peer(r)}
                pl.semaphore_signal(barrier, inc=1, device_id=there, device_id_type=MESH)

    @pl.when(sec == n_section - 1)
    def _():
        pltpu.make_async_copy(cot_ref, g_ref, copy_sem.at[0]).start()

    for weight in weights:
        weight.start()
    for i in range(owned):
        block = qkv.at[dpp * owned + i]
        block[0:SPAN, :] = q_ref[i * SPAN : (i + 1) * SPAN, :]
        block[SPAN : SPAN + NTOK, :] = kv_ref[0, i * NTOK : (i + 1) * NTOK, :]
        block[SPAN + NTOK : SPAN + 2 * NTOK, :] = kv_ref[1, i * NTOK : (i + 1) * NTOK, :]

    pl.semaphore_wait(barrier, n_dp - 1 + n_section * n_tensor - 1)

    @pl.when(sec == n_section - 1)
    def _():
        pltpu.make_async_copy(cot_ref, g_ref, copy_sem.at[0]).wait()

    key_rows = slice(SPAN, SPAN + NTOK)
    value_rows = slice(SPAN + NTOK, SPAN + 2 * NTOK)

    def head_lanes(h):
        return slice(h * HDIM, (h + 1) * HDIM)

    def share(t):
        c = span_at(t)

        @pl.when(c // owned == dpp)
        def _():
            send(qkv.at[c], qkv.at[c], qkv_send.at[c], qkv_sem.at[c], {"dp": across})
            send(qkv.at[c], qkv.at[c], qkv_send.at[c], qkv_sem.at[c], {"dp": sibling})

    def relay(t):
        c = span_at(t)

        @pl.when(c // owned == across)
        def _():
            wait_bytes(qkv.at[c], qkv_sem.at[c])
            send(qkv.at[c], qkv.at[c], qkv_send.at[c], qkv_sem.at[c], {"dp": sibling})

    def stage_a(t):
        c = span_at(t)

        @pl.when(sec < n_section - 1)
        def _():
            wait_bytes(g_ref.at[token_rows(c)], g_sem.at[c])

        out = contract_cols(g_ref[token_rows(c), :], wo_ref[...])
        pair_part[c] = out.astype(jnp.bfloat16)
        send(pair_part.at[c], pair_recv.at[c], pair_send.at[c], pair_sem.at[c], {"dp": sibling})

    def stage_a2(t):
        c = span_at(t)
        wait_bytes(pair_recv.at[c], pair_sem.at[c])
        total = pair_part[c].astype(jnp.float32) + pair_recv[c].astype(jnp.float32)
        z_part[c] = total.astype(jnp.bfloat16)
        send(z_part.at[c], z_recv.at[c], z_send.at[c], z_sem.at[c], {"dp": across})

    def stage_p(t):
        c = span_at(t)

        @pl.when(jnp.logical_and(c // owned != dpp, c // owned != across))
        def _():
            wait_bytes(qkv.at[c], qkv_sem.at[c])

        for h in range(heads):
            lanes = head_lanes(h)
            scores = contract_cols(qkv[c, 0:SPAN, lanes], qkv[c, key_rows, lanes]) * SCALE
            expo = jnp.exp(scores - jnp.max(scores, axis=-1, keepdims=True))
            prob = expo / jnp.sum(expo, axis=-1, keepdims=True)
            prob_half = prob.astype(jnp.bfloat16)
            probs[c, h] = prob
            half[c, h] = prob_half
            attended = jnp.dot(
                prob_half, qkv[c, value_rows, lanes], preferred_element_type=jnp.float32
            )
            att_ref[token_rows(c), lanes] = attended.astype(jnp.bfloat16)

    def stage_bc(t):
        c = span_at(t)
        wait_bytes(z_recv.at[c], z_sem.at[c])
        total = z_part[c].astype(jnp.float32) + z_recv[c].astype(jnp.float32)
        grad = total.astype(jnp.bfloat16)
        gatt[c] = grad
        for h in range(heads):
            lanes = head_lanes(h)
            grad_probs = contract_cols(grad[:, lanes], qkv[c, value_rows, lanes])
            prob = probs[c, h]
            delta = jnp.sum(prob * grad_probs, axis=-1, keepdims=True)
            grad_scores = (prob * (grad_probs - delta) * SCALE).astype(jnp.bfloat16)
            gscore[c, h] = grad_scores
            dq = jnp.dot(grad_scores, qkv[c, key_rows, lanes], preferred_element_type=jnp.float32)
            dq_ref[token_rows(c), lanes] = dq.astype(jnp.bfloat16)
        rows = dq_ref[token_rows(c), :]
        for r in list(range(1, n_tensor)) + [0]:
            peer = ten_peer(r)
            weight = wq_ref[pl.ds(pl.multiple_of(peer * cols, cols), cols), :]
            out = contract_cols(rows, weight)
            if r == 0:
                part_own[c] = out
            else:
                part[c, r - 1] = out.astype(jnp.bfloat16)
                send(
                    part.at[c, r - 1],
                    part_recv.at[c, r - 1],
                    part_send.at[c],
                    part_sem.at[c],
                    {"tensor": peer},
                )

    def stage_d(t):
        c = span_at(t)
        wait_bytes(part_recv.at[c], part_sem.at[c])
        total = g_ref[token_rows(c), mine].astype(jnp.float32) + part_own[c]
        for r in range(1, n_tensor):
            total = total + part_recv[c, r - 1].astype(jnp.float32)
        new_ref[c] = total.astype(jnp.bfloat16)

        @pl.when(sec > 0)
        def _():
            for r in range(n_tensor):
                send(
                    new_ref.at[c],
                    g_ref.at[token_rows(c), mine],
                    g_send.at[c],
                    g_sem.at[c],
                    {"section": sec - 1, "tensor": ten_peer(r)},
                )

        @pl.when(c != ten)
        def _():
            send(new_ref.at[c], streams_ref.at[:, mine], stream_send.at[c], stream_sem, {"tensor": c})

        @pl.when(c == ten)
        def _():
            streams_ref[:, mine] = new_ref[c]

    def stage_k(c):
        for h in range(heads):
            lanes = head_lanes(h)
            grad_k = contract_rows(gscore[c, h], qkv[c, 0:SPAN, lanes])
            dk_ref[pair_rows(c), lanes] = grad_k.astype(jnp.bfloat16)
            grad_v = contract_rows(half[c, h], gatt[c, :, lanes])
            dv_ref[pair_rows(c), lanes] = grad_v.astype(jnp.bfloat16)

    def stage_n(c):
        owner = c // share_spans
        for low in range(0, width, 512):
            block = slice(low, low + 512)
            out = contract_cols(dk_ref[pair_rows(c), :], wkv_ref[0, block, :])
            out = out + contract_cols(dv_ref[pair_rows(c), :], wkv_ref[1, block, :])
            near_part[c, :, block] = out.astype(jnp.bfloat16)

        turn = lax.rem(c, share_spans)

        @pl.when(jnp.logical_and(sec == 0, owner > 0))
        def _():
            send(
                near_part.at[c],
                front_recv.at[turn],
                near_send.at[c],
                front_sem.at[turn],
                {"section": owner},
            )

        @pl.when(jnp.logical_and(sec == 0, owner == 0))
        def _():
            front_recv[turn] = near_part[c]

        @pl.when(jnp.logical_and(sec > 0, c != ten))
        def _():
            send(
                near_part.at[c],
                plane_recv.at[lax.rem(ten - c + n_tensor, n_tensor) - 1],
                near_send.at[c],
                plane_sem,
                {"tensor": c},
            )

    last = sec == n_section - 1

    def each(count, step):
        def body(i, carry):
            step(i)
            return carry

        lax.fori_loop(0, count, body, 0)

    block_cols = 256

    def turn_inputs(j):
        block = pl.ds(pl.multiple_of(j * block_cols, block_cols), block_cols)
        in_turned[block, :] = in_ref[:, block].T
        raw_turned[block, :] = raw_ref[:, block].T
        wkv_ref[0, block, :] = pair_ref[block, 0, :]
        wkv_ref[1, block, :] = pair_ref[block, 1, :]

    def weight_grads(j):
        block = pl.ds(pl.multiple_of(j * block_cols, block_cols), block_cols)
        grad_query = jnp.dot(in_turned[block, :], dq_ref[...], preferred_element_type=jnp.float32)
        query_ref[block, :] = grad_query.astype(jnp.bfloat16)
        grad_key = jnp.dot(raw_turned[block, :], dk_ref[...], preferred_element_type=jnp.float32)
        pair_ref[block, 0, :] = grad_key.astype(jnp.bfloat16)
        grad_value = jnp.dot(raw_turned[block, :], dv_ref[...], preferred_element_type=jnp.float32)
        pair_ref[block, 1, :] = grad_value.astype(jnp.bfloat16)
        grad_outer = contract_rows(att_ref[...], g_ref[:, block])
        outer_ref[:, block] = grad_outer.astype(jnp.bfloat16)

    blocks = width // block_cols

    @pl.when(jnp.logical_not(last))
    def _():
        each(spans, share)
        each(spans, relay)
        for weight in weights:
            weight.wait()
        each(spans, stage_p)
        each(blocks, turn_inputs)

    @pl.when(last)
    def _():
        share(0)

    def tick(t, carry):
        first = t < spans
        second = jnp.logical_and(t > 0, t <= spans)

        @pl.when(first)
        def _():
            stage_a(t)

        @pl.when(t > 2)
        def _():
            stage_d(t - 3)

        @pl.when(jnp.logical_and(last, jnp.logical_and(first, t > 0)))
        def _():
            stage_p(t)

        @pl.when(first)
        def _():
            stage_a2(t)

        @pl.when(jnp.logical_and(last, t < 3))
        def _():
            @pl.when(t == 0)
            def _():
                share(1)

            share(2 * t + 2)
            share(2 * t + 3)

        @pl.when(jnp.logical_and(last, t == 0))
        def _():
            relay(0)
            stage_p(0)
            for weight in weights:
                weight.wait()

        @pl.when(jnp.logical_and(last, t < spans - 1))
        def _():
            relay(t + 1)

        @pl.when(jnp.logical_and(sec == 0, jnp.logical_and(t > 1, t < spans + 2)))
        def _():
            stage_k(span_at(t - 2))
            stage_n(span_at(t - 2))

        @pl.when(second)
        def _():
            stage_bc(t - 1)

        return carry

    lax.fori_loop(0, spans + 3, tick, 0)

    outs = [
        pltpu.make_async_copy(query_ref, query_out, copy_sem.at[0]),
        pltpu.make_async_copy(pair_ref, pair_out, copy_sem.at[1]),
        pltpu.make_async_copy(outer_ref, outer_out, copy_sem.at[2]),
        pltpu.make_async_copy(streams_ref, streams_out, copy_sem.at[5]),
    ]

    near_copy = pltpu.make_async_copy(near_ref, near_out, copy_sem.at[6])

    @pl.when(last)
    def _():
        each(blocks, turn_inputs)

    def neighbour_terms(j):
        c = lax.rem(ten + 1 + j, spans)
        stage_k(c)
        stage_n(c)

    @pl.when(sec > 0)
    def _():
        each(spans, neighbour_terms)
        each(blocks, weight_grads)
        for out in outs[:-1]:
            out.start()

    keep, quarter = near_ref.shape[0], NTOK // near_ref.shape[0]
    home = ten // share_spans
    first_peer = lax.rem(ten, share_spans) * quarter

    @pl.when(sec > 0)
    def _():
        wait_bytes(plane_recv, plane_sem)
        for piece in range(quarter):
            rows = slice(piece * keep, (piece + 1) * keep)
            total = near_part[ten, rows, :].astype(jnp.float32)
            for slot in range(n_tensor - 1):
                total = total + plane_recv[slot, rows, :].astype(jnp.float32)
            plane_sum[piece] = total.astype(jnp.bfloat16)
            here = jnp.logical_and(home == sec, first_peer + piece == ten)

            @pl.when(here)
            def _():
                far_recv[sec - 1] = plane_sum[piece]

            @pl.when(jnp.logical_not(here))
            def _():
                send(
                    plane_sum.at[piece],
                    far_recv.at[sec - 1],
                    far_send.at[piece],
                    far_sem.at[sec - 1],
                    {"section": home, "tensor": first_peer + piece},
                )

    def spread(turn):
        @pl.when(sec > 0)
        def _():
            wait_bytes(front_recv.at[turn], front_sem.at[turn])

        for step in range(quarter):
            piece = lax.rem(ten + step, quarter)
            peer = turn * quarter + piece

            @pl.when(peer != ten)
            def _():
                send(
                    front_recv.at[turn, pl.ds(pl.multiple_of(piece * keep, keep), keep)],
                    sum_recv.at[lax.rem(ten - peer + n_tensor, n_tensor) - 1],
                    sum_send,
                    sum_sem,
                    {"tensor": peer},
                )

    each(share_spans, spread)

    @pl.when(sec == 0)
    def _():
        each(blocks, weight_grads)
        for out in outs[:-1]:
            out.start()

    wait_bytes(part_recv.at[0], stream_sem)
    outs[-1].start()
    source = sec * share_spans + ten // quarter
    for slot in range(n_section - 1):

        @pl.when(jnp.logical_not(jnp.logical_and(sec == slot + 1, source == ten)))
        def _():
            wait_bytes(far_recv.at[slot], far_sem.at[slot])

    wait_bytes(sum_recv, sum_sem)
    own = pl.ds(pl.multiple_of(lax.rem(ten, quarter) * keep, keep), keep)
    total = front_recv[ten // quarter, own, :].astype(jnp.float32)
    for slot in range(n_tensor - 1):
        total = total + sum_recv[slot].astype(jnp.float32)
    for slot in range(n_section - 1):
        total = total + far_recv[slot].astype(jnp.float32)
    near_ref[...] = total.astype(jnp.bfloat16)
    near_copy.start()

    def drain(c, carry):
        wait_bytes(pair_recv.at[c], pair_send.at[c])
        wait_bytes(z_recv.at[c], z_send.at[c])
        wait_bytes(part_recv.at[c], part_send.at[c])

        @pl.when(c // owned == dpp)
        def _():
            wait_bytes(qkv.at[pl.ds(0, 2)], qkv_send.at[c])

        @pl.when(c // owned == across)
        def _():
            wait_bytes(qkv.at[c], qkv_send.at[c])

        @pl.when(jnp.logical_or(jnp.logical_and(sec == 0, c >= share_spans), jnp.logical_and(sec > 0, c != ten)))
        def _():
            wait_bytes(near_part.at[c], near_send.at[c])

        @pl.when(sec > 0)
        def _():
            wait_bytes(g_ref.at[token_rows(c)], g_send.at[c])

        @pl.when(c != ten)
        def _():
            wait_bytes(new_ref.at[c], stream_send.at[c])

        return carry

    lax.fori_loop(0, spans, drain, 0)
    wait_bytes(sum_recv, sum_send)
    for piece in range(quarter):

        @pl.when(jnp.logical_and(sec > 0, jnp.logical_not(jnp.logical_and(home == sec, first_peer + piece == ten))))
        def _():
            wait_bytes(plane_sum.at[piece], far_send.at[piece])

    for out in outs:
        out.wait()
    near_copy.wait()


def run_chain(cotangent, queries, pairs, weight_query, weight_out, weight_pair, streams_in, neighbours):
    n_section = lax.axis_size("section")
    n_tensor = lax.axis_size("tensor")
    n_dp = lax.axis_size("dp")
    total, width = cotangent.shape
    feats = queries.shape[1]
    mrows = neighbours.shape[0]
    heads = feats // HDIM
    spans = total // SPAN
    cols = width // n_tensor
    keep = mrows // (n_section * n_tensor)
    turns = spans // n_section
    bf16, f32 = jnp.bfloat16, jnp.float32
    vmem = pl.BlockSpec(memory_space=pltpu.VMEM)
    anywhere = pl.BlockSpec(memory_space=pl.ANY)
    dma = pltpu.SemaphoreType.DMA
    return pl.pallas_call(
        functools.partial(chain_kernel, n_section, n_tensor, n_dp),
        out_shape=[
            jax.ShapeDtypeStruct((SPAN, width), bf16),
            jax.ShapeDtypeStruct((keep, width), bf16),
            jax.ShapeDtypeStruct((width, feats), bf16),
            jax.ShapeDtypeStruct((width, 2, feats), bf16),
            jax.ShapeDtypeStruct((feats, width), bf16),
        ],
        in_specs=[anywhere, vmem, vmem, anywhere, vmem, anywhere, anywhere, anywhere],
        out_specs=[anywhere] * 5,
        scratch_shapes=[
            pltpu.VMEM((total, width), bf16),
            pltpu.VMEM((spans, SPAN + 2 * NTOK, feats), bf16),
            pltpu.VMEM((spans, SPAN, feats), bf16),
            pltpu.VMEM((spans, SPAN, feats), bf16),
            pltpu.VMEM((spans, SPAN, feats), bf16),
            pltpu.VMEM((spans, SPAN, feats), bf16),
            pltpu.VMEM((spans, n_tensor - 1, SPAN, cols), bf16),
            pltpu.VMEM((spans, SPAN, cols), f32),
            pltpu.VMEM((spans, n_tensor - 1, SPAN, cols), bf16),
            pltpu.VMEM((spans, SPAN, cols), bf16),
            pltpu.VMEM((SPAN, width), bf16),
            pltpu.VMEM((total, feats), bf16),
            pltpu.VMEM((total, feats), bf16),
            pltpu.VMEM((mrows, feats), bf16),
            pltpu.VMEM((mrows, feats), bf16),
            pltpu.VMEM((spans, heads, SPAN, NTOK), f32),
            pltpu.VMEM((spans, heads, SPAN, NTOK), bf16),
            pltpu.VMEM((spans, SPAN, feats), bf16),
            pltpu.VMEM((spans, heads, SPAN, NTOK), bf16),
            pltpu.VMEM((width, feats), bf16),
            pltpu.VMEM((2, width, feats), bf16),
            pltpu.VMEM((total, width), bf16),
            pltpu.VMEM((mrows, width), bf16),
            pltpu.VMEM((width, total), bf16),
            pltpu.VMEM((width, mrows), bf16),
            pltpu.VMEM((width, feats), bf16),
            pltpu.VMEM((width, 2, feats), bf16),
            pltpu.VMEM((feats, width), bf16),
            pltpu.VMEM((spans, NTOK, width), bf16),
            pltpu.VMEM((turns, NTOK, width), bf16),
            pltpu.VMEM((n_tensor - 1, NTOK, width), bf16),
            pltpu.VMEM((NTOK // keep, keep, width), bf16),
            pltpu.VMEM((n_section - 1, keep, width), bf16),
            pltpu.VMEM((n_tensor - 1, keep, width), bf16),
            pltpu.VMEM((keep, width), bf16),
            dma((7,)),
            dma((spans,)),
            dma((spans,)),
            dma((spans,)),
            dma((spans,)),
            dma((spans,)),
            dma((spans,)),
            dma((spans,)),
            dma((spans,)),
            dma((spans,)),
            dma((spans,)),
            dma((spans,)),
            dma,
            dma((spans,)),
            dma((turns,)),
            dma,
            dma((NTOK // keep,)),
            dma((n_section - 1,)),
            dma,
            dma,
        ],
        compiler_params=pltpu.CompilerParams(
            collective_id=0, has_side_effects=True, vmem_limit_bytes=60 * 2**20
        ),
    )(cotangent, queries, pairs, weight_query, weight_out, weight_pair, streams_in, neighbours)


def on_device(cotangent, queries, keys_values, streams_in, neighbours, w_query, w_key_value, w_out):
    streams, neighbour_part, grad_query, grad_pair, grad_out = run_chain(
        cotangent,
        queries[0],
        jnp.swapaxes(keys_values[0], 0, 1),
        w_query[0],
        w_out[0],
        w_key_value[0],
        streams_in[0],
        neighbours,
    )
    return (streams[None], neighbour_part, grad_query[None], grad_pair[None], grad_out[None])


def solution(mesh):
    in_specs = (
        P(None, "dp"),
        P("section", "dp", "tensor"),
        P("section", "dp", None, "tensor"),
        P("section", None, "dp"),
        P(None, "dp"),
        P("section", "dp", "tensor"),
        P("section", "dp", None, "tensor"),
        P("section", "tensor", "dp"),
    )
    out_specs = (
        P("section", "tensor", "dp"),
        P(("section", "tensor"), "dp"),
        P("section", "dp", "tensor"),
        P("section", "dp", None, "tensor"),
        P("section", "tensor", "dp"),
    )
    return jax.shard_map(
        on_device, mesh=mesh, in_specs=in_specs, out_specs=out_specs, check_vma=False
    )
```

```python
import functools

import jax
import jax.numpy as jnp
from jax import lax
from jax.experimental import pallas as pl
from jax.experimental.pallas import tpu as pltpu
from jax.sharding import PartitionSpec as P

HDIM = 128
SPAN = 64
NTOK = 128
SCALE = HDIM ** (-0.5)
MESH = pl.DeviceIdType.MESH


def contract_rows(left, right):
    return lax.dot_general(
        left, right, (((0,), (0,)), ((), ())), preferred_element_type=jnp.float32
    )


def contract_cols(left, right):
    return lax.dot_general(
        left, right, (((1,), (1,)), ((), ())), preferred_element_type=jnp.float32
    )


def wait_bytes(ref, sem):
    pltpu.make_async_copy(ref, ref, sem).wait()


def chain_kernel(
    n_section,
    n_tensor,
    n_dp,
    cot_ref,
    q_ref,
    kv_ref,
    wq_hbm,
    wo_ref,
    wkv_hbm,
    in_hbm,
    near_hbm,
    streams_out,
    near_out,
    query_out,
    pair_out,
    outer_out,
    g_ref,
    qkv,
    pair_part,
    pair_recv,
    z_part,
    z_recv,
    part,
    part_own,
    part_recv,
    new_ref,
    streams_ref,
    dq_ref,
    att_ref,
    dk_ref,
    dv_ref,
    probs,
    half,
    gatt,
    gscore,
    wq_ref,
    wkv_ref,
    in_ref,
    raw_ref,
    in_turned,
    raw_turned,
    query_ref,
    pair_ref,
    outer_ref,
    near_part,
    front_recv,
    plane_recv,
    plane_sum,
    far_recv,
    sum_recv,
    near_ref,
    copy_sem,
    qkv_send,
    qkv_sem,
    pair_send,
    pair_sem,
    z_send,
    z_sem,
    part_send,
    part_sem,
    g_send,
    g_sem,
    stream_send,
    stream_sem,
    near_send,
    front_sem,
    plane_sem,
    far_send,
    far_sem,
    sum_send,
    sum_sem,
):
    sec = lax.axis_index("section")
    ten = lax.axis_index("tensor")
    dpp = lax.axis_index("dp")
    width = g_ref.shape[1]
    spans = g_ref.shape[0] // SPAN
    owned = spans // n_dp
    cols = width // n_tensor
    feats = q_ref.shape[1]
    heads = feats // HDIM
    mine = pl.ds(pl.multiple_of(ten * cols, cols), cols)
    sibling = dpp + 1 - 2 * lax.rem(dpp, 2)
    across = lax.rem(dpp + 2, n_dp)

    def dp_peer(r):
        return lax.rem(dpp + r, n_dp)

    def ten_peer(r):
        return lax.rem(ten + r, n_tensor)

    share_spans = spans // n_section
    weights = [
        pltpu.make_async_copy(wq_hbm, wq_ref, copy_sem.at[1]),
        pltpu.make_async_copy(wkv_hbm, pair_ref, copy_sem.at[2]),
        pltpu.make_async_copy(in_hbm, in_ref, copy_sem.at[3]),
        pltpu.make_async_copy(near_hbm, raw_ref, copy_sem.at[4]),
    ]

    def span_at(t):
        return lax.rem(t + owned, spans)

    def token_rows(c):
        return pl.ds(pl.multiple_of(c * SPAN, SPAN), SPAN)

    def pair_rows(c):
        return pl.ds(pl.multiple_of(c * NTOK, NTOK), NTOK)

    def send(src, dst, send_sem, recv_sem, device):
        pltpu.make_async_remote_copy(
            src_ref=src,
            dst_ref=dst,
            send_sem=send_sem,
            recv_sem=recv_sem,
            device_id=device,
            device_id_type=MESH,
        ).start()

    barrier = pltpu.get_barrier_semaphore()
    for r in range(1, n_dp):
        pl.semaphore_signal(barrier, inc=1, device_id={"dp": dp_peer(r)}, device_id_type=MESH)
    for step in range(n_section):
        for r in range(n_tensor):
            if step or r:
                there = {"section": lax.rem(sec + step, n_section), "tensor": ten_peer(r)}
                pl.semaphore_signal(barrier, inc=1, device_id=there, device_id_type=MESH)

    @pl.when(sec == n_section - 1)
    def _():
        pltpu.make_async_copy(cot_ref, g_ref, copy_sem.at[0]).start()

    for weight in weights:
        weight.start()
    for i in range(owned):
        block = qkv.at[dpp * owned + i]
        block[0:SPAN, :] = q_ref[i * SPAN : (i + 1) * SPAN, :]
        block[SPAN : SPAN + NTOK, :] = kv_ref[0, i * NTOK : (i + 1) * NTOK, :]
        block[SPAN + NTOK : SPAN + 2 * NTOK, :] = kv_ref[1, i * NTOK : (i + 1) * NTOK, :]

    pl.semaphore_wait(barrier, n_dp - 1 + n_section * n_tensor - 1)

    @pl.when(sec == n_section - 1)
    def _():
        pltpu.make_async_copy(cot_ref, g_ref, copy_sem.at[0]).wait()

    key_rows = slice(SPAN, SPAN + NTOK)
    value_rows = slice(SPAN + NTOK, SPAN + 2 * NTOK)

    def head_lanes(h):
        return slice(h * HDIM, (h + 1) * HDIM)

    def share(t):
        c = span_at(t)

        @pl.when(c // owned == dpp)
        def _():
            send(qkv.at[c], qkv.at[c], qkv_send.at[c], qkv_sem.at[c], {"dp": across})
            send(qkv.at[c], qkv.at[c], qkv_send.at[c], qkv_sem.at[c], {"dp": sibling})

    def relay(t):
        c = span_at(t)

        @pl.when(c // owned == across)
        def _():
            wait_bytes(qkv.at[c], qkv_sem.at[c])
            send(qkv.at[c], qkv.at[c], qkv_send.at[c], qkv_sem.at[c], {"dp": sibling})

    def stage_a(t):
        c = span_at(t)

        @pl.when(sec < n_section - 1)
        def _():
            wait_bytes(g_ref.at[token_rows(c)], g_sem.at[c])

        out = contract_cols(g_ref[token_rows(c), :], wo_ref[...])
        pair_part[c] = out.astype(jnp.bfloat16)
        send(pair_part.at[c], pair_recv.at[c], pair_send.at[c], pair_sem.at[c], {"dp": sibling})

    def stage_a2(t):
        c = span_at(t)
        wait_bytes(pair_recv.at[c], pair_sem.at[c])
        total = pair_part[c].astype(jnp.float32) + pair_recv[c].astype(jnp.float32)
        z_part[c] = total.astype(jnp.bfloat16)
        send(z_part.at[c], z_recv.at[c], z_send.at[c], z_sem.at[c], {"dp": across})

    def stage_p(t):
        c = span_at(t)

        @pl.when(jnp.logical_and(c // owned != dpp, c // owned != across))
        def _():
            wait_bytes(qkv.at[c], qkv_sem.at[c])

        lanes = [head_lanes(h) for h in range(heads)]
        scores = [
            contract_cols(qkv[c, 0:SPAN, lane], qkv[c, key_rows, lane]) * SCALE for lane in lanes
        ]
        expo = [jnp.exp(x - jnp.max(x, axis=-1, keepdims=True)) for x in scores]
        prob = [x / jnp.sum(x, axis=-1, keepdims=True) for x in expo]
        prob_half = [x.astype(jnp.bfloat16) for x in prob]
        attended = [
            jnp.dot(x, qkv[c, value_rows, lane], preferred_element_type=jnp.float32)
            for x, lane in zip(prob_half, lanes)
        ]
        for h in range(heads):
            probs[c, h] = prob[h]
            half[c, h] = prob_half[h]
            att_ref[token_rows(c), lanes[h]] = attended[h].astype(jnp.bfloat16)

    def stage_bc(t):
        c = span_at(t)
        wait_bytes(z_recv.at[c], z_sem.at[c])
        total = z_part[c].astype(jnp.float32) + z_recv[c].astype(jnp.float32)
        grad = total.astype(jnp.bfloat16)
        lanes = [head_lanes(h) for h in range(heads)]
        prob = [probs[c, h] for h in range(heads)]
        grad_probs = [contract_cols(grad[:, lane], qkv[c, value_rows, lane]) for lane in lanes]
        delta = [jnp.sum(p * x, axis=-1, keepdims=True) for p, x in zip(prob, grad_probs)]
        grad_scores = [
            (p * (x - d) * SCALE).astype(jnp.bfloat16) for p, x, d in zip(prob, grad_probs, delta)
        ]
        dq = [
            jnp.dot(x, qkv[c, key_rows, lane], preferred_element_type=jnp.float32)
            for x, lane in zip(grad_scores, lanes)
        ]
        rows = jnp.concatenate([x.astype(jnp.bfloat16) for x in dq], axis=1)
        for r in list(range(1, n_tensor)) + [0]:
            peer = ten_peer(r)
            weight = wq_ref[pl.ds(pl.multiple_of(peer * cols, cols), cols), :]
            out = contract_cols(rows, weight)
            if r == 0:
                part_own[c] = out
            else:
                part[c, r - 1] = out.astype(jnp.bfloat16)
        for r in range(1, n_tensor):
            send(
                part.at[c, r - 1],
                part_recv.at[c, r - 1],
                part_send.at[c],
                part_sem.at[c],
                {"tensor": ten_peer(r)},
            )
        gatt[c] = grad
        dq_ref[token_rows(c), :] = rows
        for h in range(heads):
            gscore[c, h] = grad_scores[h]

    def stage_d(t):
        c = span_at(t)
        wait_bytes(part_recv.at[c], part_sem.at[c])
        total = g_ref[token_rows(c), mine].astype(jnp.float32) + part_own[c]
        for r in range(1, n_tensor):
            total = total + part_recv[c, r - 1].astype(jnp.float32)
        new_ref[c] = total.astype(jnp.bfloat16)

        @pl.when(sec > 0)
        def _():
            for r in range(n_tensor):
                send(
                    new_ref.at[c],
                    g_ref.at[token_rows(c), mine],
                    g_send.at[c],
                    g_sem.at[c],
                    {"section": sec - 1, "tensor": ten_peer(r)},
                )

    def stage_s(j):
        c = lax.rem(ten + 1 + j, spans)

        @pl.when(c != ten)
        def _():
            send(new_ref.at[c], streams_ref.at[:, mine], stream_send.at[c], stream_sem, {"tensor": c})

        @pl.when(c == ten)
        def _():
            streams_ref[:, mine] = new_ref[c]

    def stage_k(c):
        for h in range(heads):
            lanes = head_lanes(h)
            grad_k = contract_rows(gscore[c, h], qkv[c, 0:SPAN, lanes])
            dk_ref[pair_rows(c), lanes] = grad_k.astype(jnp.bfloat16)
            grad_v = contract_rows(half[c, h], gatt[c, :, lanes])
            dv_ref[pair_rows(c), lanes] = grad_v.astype(jnp.bfloat16)

    def even(i):
        return lax.rem(i, 2) == 0

    def by_plane(owner):
        return jnp.logical_or(sec > 1, jnp.logical_and(sec == 1, jnp.logical_not(even(owner))))

    def stage_n(c):
        owner = c // share_spans
        for low in range(0, width, 512):
            block = slice(low, low + 512)
            out = contract_cols(dk_ref[pair_rows(c), :], wkv_ref[0, block, :])
            out = out + contract_cols(dv_ref[pair_rows(c), :], wkv_ref[1, block, :])
            near_part[c, :, block] = out.astype(jnp.bfloat16)

        turn = lax.rem(c, share_spans)

        @pl.when(jnp.logical_and(sec == 0, owner > 0))
        def _():
            send(
                near_part.at[c],
                front_recv.at[0, turn],
                near_send.at[c],
                front_sem.at[0, turn],
                {"section": owner},
            )

        @pl.when(jnp.logical_and(sec == 1, even(owner)))
        def _():
            send(
                near_part.at[c],
                front_recv.at[1, turn],
                near_send.at[c],
                front_sem.at[1, turn],
                {"section": owner},
            )

        @pl.when(jnp.logical_and(sec == 0, owner == 0))
        def _():
            front_recv[0, turn] = near_part[c]

        @pl.when(jnp.logical_and(by_plane(owner), c != ten))
        def _():
            send(
                near_part.at[c],
                plane_recv.at[lax.rem(ten - c + n_tensor, n_tensor) - 1],
                near_send.at[c],
                plane_sem,
                {"tensor": c},
            )

    last = sec == n_section - 1

    def each(count, step):
        def body(i, carry):
            step(i)
            return carry

        lax.fori_loop(0, count, body, 0)

    block_cols = 256

    def turn_inputs(j):
        block = pl.ds(pl.multiple_of(j * block_cols, block_cols), block_cols)
        in_turned[block, :] = in_ref[:, block].T
        raw_turned[block, :] = raw_ref[:, block].T
        wkv_ref[0, block, :] = pair_ref[block, 0, :]
        wkv_ref[1, block, :] = pair_ref[block, 1, :]

    def weight_grads(j):
        block = pl.ds(pl.multiple_of(j * block_cols, block_cols), block_cols)
        grad_query = jnp.dot(in_turned[block, :], dq_ref[...], preferred_element_type=jnp.float32)
        query_ref[block, :] = grad_query.astype(jnp.bfloat16)
        grad_key = jnp.dot(raw_turned[block, :], dk_ref[...], preferred_element_type=jnp.float32)
        pair_ref[block, 0, :] = grad_key.astype(jnp.bfloat16)
        grad_value = jnp.dot(raw_turned[block, :], dv_ref[...], preferred_element_type=jnp.float32)
        pair_ref[block, 1, :] = grad_value.astype(jnp.bfloat16)
        grad_outer = contract_rows(att_ref[...], g_ref[:, block])
        outer_ref[:, block] = grad_outer.astype(jnp.bfloat16)

    blocks = width // block_cols

    @pl.when(jnp.logical_not(last))
    def _():
        each(spans, share)
        each(spans, relay)
        for weight in weights:
            weight.wait()
        each(spans, stage_p)
        each(blocks, turn_inputs)

    @pl.when(last)
    def _():
        share(0)

    def tick(t, carry):
        first = t < spans
        second = jnp.logical_and(t > 0, t <= spans)

        @pl.when(first)
        def _():
            stage_a(t)

        @pl.when(t > 2)
        def _():
            stage_d(t - 3)

        @pl.when(jnp.logical_and(last, jnp.logical_and(first, t > 0)))
        def _():
            stage_p(t)

        @pl.when(first)
        def _():
            stage_a2(t)

        @pl.when(jnp.logical_and(last, t < 3))
        def _():
            @pl.when(t == 0)
            def _():
                share(1)

            share(2 * t + 2)
            share(2 * t + 3)

        @pl.when(jnp.logical_and(last, t == 0))
        def _():
            relay(0)
            stage_p(0)
            for weight in weights:
                weight.wait()

        @pl.when(jnp.logical_and(last, t < spans - 1))
        def _():
            relay(t + 1)

        @pl.when(jnp.logical_and(sec == 0, jnp.logical_and(t > 1, t < spans + 2)))
        def _():
            stage_k(span_at(t - 2))
            stage_n(span_at(t - 2))

        @pl.when(second)
        def _():
            stage_bc(t - 1)

        return carry

    lax.fori_loop(0, spans + 3, tick, 0)

    outs = [
        pltpu.make_async_copy(query_ref, query_out, copy_sem.at[0]),
        pltpu.make_async_copy(pair_ref, pair_out, copy_sem.at[1]),
        pltpu.make_async_copy(outer_ref, outer_out, copy_sem.at[2]),
        pltpu.make_async_copy(streams_ref, streams_out, copy_sem.at[5]),
    ]

    near_copy = pltpu.make_async_copy(near_ref, near_out, copy_sem.at[6])

    @pl.when(sec > 0)
    def _():
        each(spans, stage_s)

    @pl.when(last)
    def _():
        each(blocks, turn_inputs)

    def neighbour_terms(j):
        c = lax.rem(ten + 1 + j, spans)
        stage_k(c)
        stage_n(c)

    @pl.when(sec > 0)
    def _():
        each(spans, neighbour_terms)
        each(blocks, weight_grads)
        for out in outs[:-1]:
            out.start()

    keep, quarter = near_ref.shape[0], NTOK // near_ref.shape[0]
    home = ten // share_spans
    first_peer = lax.rem(ten, share_spans) * quarter

    @pl.when(by_plane(home))
    def _():
        wait_bytes(plane_recv, plane_sem)
        for piece in range(quarter):
            rows = slice(piece * keep, (piece + 1) * keep)
            total = near_part[ten, rows, :].astype(jnp.float32)
            for slot in range(n_tensor - 1):
                total = total + plane_recv[slot, rows, :].astype(jnp.float32)
            plane_sum[piece] = total.astype(jnp.bfloat16)
            here = jnp.logical_and(home == sec, first_peer + piece == ten)

            @pl.when(here)
            def _():
                far_recv[sec - 1] = plane_sum[piece]

            @pl.when(jnp.logical_not(here))
            def _():
                send(
                    plane_sum.at[piece],
                    far_recv.at[sec - 1],
                    far_send.at[piece],
                    far_sem.at[sec - 1],
                    {"section": home, "tensor": first_peer + piece},
                )

    def spread(turn):
        @pl.when(sec > 0)
        def _():
            wait_bytes(front_recv.at[0, turn], front_sem.at[0, turn])

        @pl.when(even(sec))
        def _():
            wait_bytes(front_recv.at[1, turn], front_sem.at[1, turn])
            for piece in range(quarter):
                rows = slice(piece * keep, (piece + 1) * keep)
                total = front_recv[0, turn, rows, :].astype(jnp.float32)
                total = total + front_recv[1, turn, rows, :].astype(jnp.float32)
                front_recv[0, turn, rows, :] = total.astype(jnp.bfloat16)

        for step in range(quarter):
            piece = lax.rem(ten + step, quarter)
            peer = turn * quarter + piece

            @pl.when(peer != ten)
            def _():
                send(
                    front_recv.at[0, turn, pl.ds(pl.multiple_of(piece * keep, keep), keep)],
                    sum_recv.at[lax.rem(ten - peer + n_tensor, n_tensor) - 1],
                    sum_send,
                    sum_sem,
                    {"tensor": peer},
                )

    each(share_spans, spread)

    @pl.when(sec == 0)
    def _():
        each(spans, stage_s)
        each(blocks, weight_grads)
        for out in outs[:-1]:
            out.start()

    @pl.when(even(sec))
    def _():
        far_recv[0] = jnp.zeros(far_recv.shape[1:], far_recv.dtype)

    wait_bytes(part_recv.at[0], stream_sem)
    outs[-1].start()
    source = sec * share_spans + ten // quarter
    for slot in range(n_section - 1):

        comes = jnp.logical_not(jnp.logical_and(sec == slot + 1, source == ten))
        if slot == 0:
            comes = jnp.logical_and(comes, jnp.logical_not(even(sec)))

        @pl.when(comes)
        def _():
            wait_bytes(far_recv.at[slot], far_sem.at[slot])

    wait_bytes(sum_recv, sum_sem)
    own = pl.ds(pl.multiple_of(lax.rem(ten, quarter) * keep, keep), keep)
    total = front_recv[0, ten // quarter, own, :].astype(jnp.float32)
    for slot in range(n_tensor - 1):
        total = total + sum_recv[slot].astype(jnp.float32)
    for slot in range(n_section - 1):
        total = total + far_recv[slot].astype(jnp.float32)
    near_ref[...] = total.astype(jnp.bfloat16)
    near_copy.start()

    def drain(c, carry):
        wait_bytes(pair_recv.at[c], pair_send.at[c])
        wait_bytes(z_recv.at[c], z_send.at[c])
        wait_bytes(part_recv.at[c], part_send.at[c])

        @pl.when(c // owned == dpp)
        def _():
            wait_bytes(qkv.at[pl.ds(0, 2)], qkv_send.at[c])

        @pl.when(c // owned == across)
        def _():
            wait_bytes(qkv.at[c], qkv_send.at[c])

        owner = c // share_spans
        front = jnp.logical_or(
            jnp.logical_and(sec == 0, owner > 0), jnp.logical_and(sec == 1, even(owner))
        )

        @pl.when(jnp.logical_or(front, jnp.logical_and(by_plane(owner), c != ten)))
        def _():
            wait_bytes(near_part.at[c], near_send.at[c])

        @pl.when(sec > 0)
        def _():
            wait_bytes(g_ref.at[token_rows(c)], g_send.at[c])

        @pl.when(c != ten)
        def _():
            wait_bytes(new_ref.at[c], stream_send.at[c])

        return carry

    lax.fori_loop(0, spans, drain, 0)
    wait_bytes(sum_recv, sum_send)
    for piece in range(quarter):

        @pl.when(jnp.logical_and(by_plane(home), jnp.logical_not(jnp.logical_and(home == sec, first_peer + piece == ten))))
        def _():
            wait_bytes(plane_sum.at[piece], far_send.at[piece])

    for out in outs:
        out.wait()
    near_copy.wait()


def run_chain(cotangent, queries, pairs, weight_query, weight_out, weight_pair, streams_in, neighbours):
    n_section = lax.axis_size("section")
    n_tensor = lax.axis_size("tensor")
    n_dp = lax.axis_size("dp")
    total, width = cotangent.shape
    feats = queries.shape[1]
    mrows = neighbours.shape[0]
    heads = feats // HDIM
    spans = total // SPAN
    cols = width // n_tensor
    keep = mrows // (n_section * n_tensor)
    turns = spans // n_section
    bf16, f32 = jnp.bfloat16, jnp.float32
    vmem = pl.BlockSpec(memory_space=pltpu.VMEM)
    anywhere = pl.BlockSpec(memory_space=pl.ANY)
    dma = pltpu.SemaphoreType.DMA
    return pl.pallas_call(
        functools.partial(chain_kernel, n_section, n_tensor, n_dp),
        out_shape=[
            jax.ShapeDtypeStruct((SPAN, width), bf16),
            jax.ShapeDtypeStruct((keep, width), bf16),
            jax.ShapeDtypeStruct((width, feats), bf16),
            jax.ShapeDtypeStruct((width, 2, feats), bf16),
            jax.ShapeDtypeStruct((feats, width), bf16),
        ],
        in_specs=[anywhere, vmem, vmem, anywhere, vmem, anywhere, anywhere, anywhere],
        out_specs=[anywhere] * 5,
        scratch_shapes=[
            pltpu.VMEM((total, width), bf16),
            pltpu.VMEM((spans, SPAN + 2 * NTOK, feats), bf16),
            pltpu.VMEM((spans, SPAN, feats), bf16),
            pltpu.VMEM((spans, SPAN, feats), bf16),
            pltpu.VMEM((spans, SPAN, feats), bf16),
            pltpu.VMEM((spans, SPAN, feats), bf16),
            pltpu.VMEM((spans, n_tensor - 1, SPAN, cols), bf16),
            pltpu.VMEM((spans, SPAN, cols), f32),
            pltpu.VMEM((spans, n_tensor - 1, SPAN, cols), bf16),
            pltpu.VMEM((spans, SPAN, cols), bf16),
            pltpu.VMEM((SPAN, width), bf16),
            pltpu.VMEM((total, feats), bf16),
            pltpu.VMEM((total, feats), bf16),
            pltpu.VMEM((mrows, feats), bf16),
            pltpu.VMEM((mrows, feats), bf16),
            pltpu.VMEM((spans, heads, SPAN, NTOK), f32),
            pltpu.VMEM((spans, heads, SPAN, NTOK), bf16),
            pltpu.VMEM((spans, SPAN, feats), bf16),
            pltpu.VMEM((spans, heads, SPAN, NTOK), bf16),
            pltpu.VMEM((width, feats), bf16),
            pltpu.VMEM((2, width, feats), bf16),
            pltpu.VMEM((total, width), bf16),
            pltpu.VMEM((mrows, width), bf16),
            pltpu.VMEM((width, total), bf16),
            pltpu.VMEM((width, mrows), bf16),
            pltpu.VMEM((width, feats), bf16),
            pltpu.VMEM((width, 2, feats), bf16),
            pltpu.VMEM((feats, width), bf16),
            pltpu.VMEM((spans, NTOK, width), bf16),
            pltpu.VMEM((2, turns, NTOK, width), bf16),
            pltpu.VMEM((n_tensor - 1, NTOK, width), bf16),
            pltpu.VMEM((NTOK // keep, keep, width), bf16),
            pltpu.VMEM((n_section - 1, keep, width), bf16),
            pltpu.VMEM((n_tensor - 1, keep, width), bf16),
            pltpu.VMEM((keep, width), bf16),
            dma((7,)),
            dma((spans,)),
            dma((spans,)),
            dma((spans,)),
            dma((spans,)),
            dma((spans,)),
            dma((spans,)),
            dma((spans,)),
            dma((spans,)),
            dma((spans,)),
            dma((spans,)),
            dma((spans,)),
            dma,
            dma((spans,)),
            dma((2, turns)),
            dma,
            dma((NTOK // keep,)),
            dma((n_section - 1,)),
            dma,
            dma,
        ],
        compiler_params=pltpu.CompilerParams(
            collective_id=0, has_side_effects=True, vmem_limit_bytes=60 * 2**20
        ),
    )(cotangent, queries, pairs, weight_query, weight_out, weight_pair, streams_in, neighbours)


def on_device(cotangent, queries, keys_values, streams_in, neighbours, w_query, w_key_value, w_out):
    streams, neighbour_part, grad_query, grad_pair, grad_out = run_chain(
        cotangent,
        queries[0],
        jnp.swapaxes(keys_values[0], 0, 1),
        w_query[0],
        w_out[0],
        w_key_value[0],
        streams_in[0],
        neighbours,
    )
    return (streams[None], neighbour_part, grad_query[None], grad_pair[None], grad_out[None])


def solution(mesh):
    in_specs = (
        P(None, "dp"),
        P("section", "dp", "tensor"),
        P("section", "dp", None, "tensor"),
        P("section", None, "dp"),
        P(None, "dp"),
        P("section", "dp", "tensor"),
        P("section", "dp", None, "tensor"),
        P("section", "tensor", "dp"),
    )
    out_specs = (
        P("section", "tensor", "dp"),
        P(("section", "tensor"), "dp"),
        P("section", "dp", "tensor"),
        P("section", "dp", None, "tensor"),
        P("section", "tensor", "dp"),
    )
    return jax.shard_map(
        on_device, mesh=mesh, in_specs=in_specs, out_specs=out_specs, check_vma=False
    )
```

```python
import functools

import jax
import jax.numpy as jnp
from jax import lax
from jax.experimental import pallas as pl
from jax.experimental.pallas import tpu as pltpu
from jax.sharding import PartitionSpec as P

HDIM = 128
SPAN = 64
NTOK = 128
SCALE = HDIM ** (-0.5)
MESH = pl.DeviceIdType.MESH


def contract_rows(left, right):
    return lax.dot_general(
        left, right, (((0,), (0,)), ((), ())), preferred_element_type=jnp.float32
    )


def contract_cols(left, right):
    return lax.dot_general(
        left, right, (((1,), (1,)), ((), ())), preferred_element_type=jnp.float32
    )


def wait_bytes(ref, sem):
    pltpu.make_async_copy(ref, ref, sem).wait()


def chain_kernel(
    n_section,
    n_tensor,
    n_dp,
    cot_ref,
    q_ref,
    kv_ref,
    wq_hbm,
    wo_ref,
    wkv_hbm,
    in_hbm,
    near_hbm,
    streams_out,
    near_out,
    query_out,
    pair_out,
    outer_out,
    g_ref,
    qkv,
    pair_part,
    pair_recv,
    z_part,
    z_recv,
    part,
    part_own,
    part_recv,
    new_ref,
    streams_ref,
    dq_ref,
    att_ref,
    dk_ref,
    dv_ref,
    probs,
    half,
    gatt,
    gscore,
    wq_ref,
    wkv_ref,
    in_ref,
    raw_ref,
    in_turned,
    raw_turned,
    query_ref,
    pair_ref,
    outer_ref,
    near_part,
    front_recv,
    plane_recv,
    plane_sum,
    far_recv,
    sum_recv,
    near_ref,
    copy_sem,
    qkv_send,
    qkv_sem,
    pair_send,
    pair_sem,
    z_send,
    z_sem,
    part_send,
    part_sem,
    g_send,
    g_sem,
    stream_send,
    stream_sem,
    near_send,
    front_sem,
    plane_sem,
    far_send,
    far_sem,
    sum_send,
    sum_sem,
):
    sec = lax.axis_index("section")
    ten = lax.axis_index("tensor")
    dpp = lax.axis_index("dp")
    width = g_ref.shape[1]
    spans = g_ref.shape[0] // SPAN
    owned = spans // n_dp
    cols = width // n_tensor
    feats = q_ref.shape[1]
    heads = feats // HDIM
    mine = pl.ds(pl.multiple_of(ten * cols, cols), cols)
    sibling = dpp + 1 - 2 * lax.rem(dpp, 2)
    across = lax.rem(dpp + 2, n_dp)

    def dp_peer(r):
        return lax.rem(dpp + r, n_dp)

    def ten_peer(r):
        return lax.rem(ten + r, n_tensor)

    share_spans = spans // n_section
    weights = [
        pltpu.make_async_copy(wq_hbm, wq_ref, copy_sem.at[1]),
        pltpu.make_async_copy(wkv_hbm, pair_ref, copy_sem.at[2]),
        pltpu.make_async_copy(in_hbm, in_ref, copy_sem.at[3]),
        pltpu.make_async_copy(near_hbm, raw_ref, copy_sem.at[4]),
    ]

    def span_at(t):
        return lax.rem(t + owned, spans)

    def token_rows(c):
        return pl.ds(pl.multiple_of(c * SPAN, SPAN), SPAN)

    def pair_rows(c):
        return pl.ds(pl.multiple_of(c * NTOK, NTOK), NTOK)

    def send(src, dst, send_sem, recv_sem, device):
        pltpu.make_async_remote_copy(
            src_ref=src,
            dst_ref=dst,
            send_sem=send_sem,
            recv_sem=recv_sem,
            device_id=device,
            device_id_type=MESH,
        ).start()

    barrier = pltpu.get_barrier_semaphore()
    for r in range(1, n_dp):
        pl.semaphore_signal(barrier, inc=1, device_id={"dp": dp_peer(r)}, device_id_type=MESH)
    for step in range(n_section):
        for r in range(n_tensor):
            if step or r:
                there = {"section": lax.rem(sec + step, n_section), "tensor": ten_peer(r)}
                pl.semaphore_signal(barrier, inc=1, device_id=there, device_id_type=MESH)

    @pl.when(sec == n_section - 1)
    def _():
        pltpu.make_async_copy(cot_ref, g_ref, copy_sem.at[0]).start()

    for weight in weights:
        weight.start()
    for i in range(owned):
        block = qkv.at[dpp * owned + i]
        block[0:SPAN, :] = q_ref[i * SPAN : (i + 1) * SPAN, :]
        block[SPAN : SPAN + NTOK, :] = kv_ref[0, i * NTOK : (i + 1) * NTOK, :]
        block[SPAN + NTOK : SPAN + 2 * NTOK, :] = kv_ref[1, i * NTOK : (i + 1) * NTOK, :]

    pl.semaphore_wait(barrier, n_dp - 1 + n_section * n_tensor - 1)

    @pl.when(sec == n_section - 1)
    def _():
        pltpu.make_async_copy(cot_ref, g_ref, copy_sem.at[0]).wait()

    key_rows = slice(SPAN, SPAN + NTOK)
    value_rows = slice(SPAN + NTOK, SPAN + 2 * NTOK)

    def head_lanes(h):
        return slice(h * HDIM, (h + 1) * HDIM)

    def share(t):
        c = span_at(t)

        @pl.when(c // owned == dpp)
        def _():
            send(qkv.at[c], qkv.at[c], qkv_send.at[c], qkv_sem.at[c], {"dp": across})
            send(qkv.at[c], qkv.at[c], qkv_send.at[c], qkv_sem.at[c], {"dp": sibling})

    def relay(t):
        c = span_at(t)

        @pl.when(c // owned == across)
        def _():
            wait_bytes(qkv.at[c], qkv_sem.at[c])
            send(qkv.at[c], qkv.at[c], qkv_send.at[c], qkv_sem.at[c], {"dp": sibling})

    def stage_a(t):
        c = span_at(t)

        @pl.when(sec < n_section - 1)
        def _():
            wait_bytes(g_ref.at[token_rows(c)], g_sem.at[c])

        out = contract_cols(g_ref[token_rows(c), :], wo_ref[...])
        pair_part[c] = out.astype(jnp.bfloat16)
        send(pair_part.at[c], pair_recv.at[c], pair_send.at[c], pair_sem.at[c], {"dp": sibling})

    def stage_a2(t):
        c = span_at(t)
        wait_bytes(pair_recv.at[c], pair_sem.at[c])
        total = pair_part[c].astype(jnp.float32) + pair_recv[c].astype(jnp.float32)
        z_part[c] = total.astype(jnp.bfloat16)
        send(z_part.at[c], z_recv.at[c], z_send.at[c], z_sem.at[c], {"dp": across})

    def stage_p(t):
        c = span_at(t)

        @pl.when(jnp.logical_and(c // owned != dpp, c // owned != across))
        def _():
            wait_bytes(qkv.at[c], qkv_sem.at[c])

        lanes = [head_lanes(h) for h in range(heads)]
        scores = [
            contract_cols(qkv[c, 0:SPAN, lane], qkv[c, key_rows, lane]) * SCALE for lane in lanes
        ]
        expo = [jnp.exp(x - jnp.max(x, axis=-1, keepdims=True)) for x in scores]
        prob = [x / jnp.sum(x, axis=-1, keepdims=True) for x in expo]
        prob_half = [x.astype(jnp.bfloat16) for x in prob]
        attended = [
            jnp.dot(x, qkv[c, value_rows, lane], preferred_element_type=jnp.float32)
            for x, lane in zip(prob_half, lanes)
        ]
        for h in range(heads):
            probs[c, h] = prob[h]
            half[c, h] = prob_half[h]
            att_ref[token_rows(c), lanes[h]] = attended[h].astype(jnp.bfloat16)

    def stage_bc(t):
        c = span_at(t)
        wait_bytes(z_recv.at[c], z_sem.at[c])
        total = z_part[c].astype(jnp.float32) + z_recv[c].astype(jnp.float32)
        grad = total.astype(jnp.bfloat16)
        lanes = [head_lanes(h) for h in range(heads)]
        prob = [probs[c, h] for h in range(heads)]
        grad_probs = [contract_cols(grad[:, lane], qkv[c, value_rows, lane]) for lane in lanes]
        delta = [jnp.sum(p * x, axis=-1, keepdims=True) for p, x in zip(prob, grad_probs)]
        grad_scores = [
            (p * (x - d) * SCALE).astype(jnp.bfloat16) for p, x, d in zip(prob, grad_probs, delta)
        ]
        dq = [
            jnp.dot(x, qkv[c, key_rows, lane], preferred_element_type=jnp.float32)
            for x, lane in zip(grad_scores, lanes)
        ]
        rows = jnp.concatenate([x.astype(jnp.bfloat16) for x in dq], axis=1)
        for r in list(range(1, n_tensor)) + [0]:
            peer = ten_peer(r)
            weight = wq_ref[pl.ds(pl.multiple_of(peer * cols, cols), cols), :]
            out = contract_cols(rows, weight)
            if r == 0:
                part_own[c] = out
            else:
                part[c, r - 1] = out.astype(jnp.bfloat16)
        for r in range(1, n_tensor):
            send(
                part.at[c, r - 1],
                part_recv.at[c, r - 1],
                part_send.at[c],
                part_sem.at[c],
                {"tensor": ten_peer(r)},
            )
        gatt[c] = grad
        dq_ref[token_rows(c), :] = rows
        for h in range(heads):
            gscore[c, h] = grad_scores[h]

    def stage_d(t):
        c = span_at(t)
        wait_bytes(part_recv.at[c], part_sem.at[c])
        total = g_ref[token_rows(c), mine].astype(jnp.float32) + part_own[c]
        for r in range(1, n_tensor):
            total = total + part_recv[c, r - 1].astype(jnp.float32)
        new_ref[c] = total.astype(jnp.bfloat16)

        @pl.when(sec > 0)
        def _():
            for r in range(n_tensor):
                send(
                    new_ref.at[c],
                    g_ref.at[token_rows(c), mine],
                    g_send.at[c],
                    g_sem.at[c],
                    {"section": sec - 1, "tensor": ten_peer(r)},
                )

    def stage_s(j):
        c = lax.rem(ten + 1 + j, spans)

        @pl.when(c != ten)
        def _():
            send(new_ref.at[c], streams_ref.at[:, mine], stream_send.at[c], stream_sem, {"tensor": c})

        @pl.when(c == ten)
        def _():
            streams_ref[:, mine] = new_ref[c]

    def stage_k(c):
        for h in range(heads):
            lanes = head_lanes(h)
            grad_k = contract_rows(gscore[c, h], qkv[c, 0:SPAN, lanes])
            dk_ref[pair_rows(c), lanes] = grad_k.astype(jnp.bfloat16)
            grad_v = contract_rows(half[c, h], gatt[c, :, lanes])
            dv_ref[pair_rows(c), lanes] = grad_v.astype(jnp.bfloat16)

    def even(i):
        return lax.rem(i, 2) == 0

    def by_plane(owner):
        return jnp.logical_or(sec > 1, jnp.logical_and(sec == 1, jnp.logical_not(even(owner))))

    def stage_n(c):
        owner = c // share_spans
        for low in range(0, width, 512):
            block = slice(low, low + 512)
            out = contract_cols(dk_ref[pair_rows(c), :], wkv_ref[0, block, :])
            out = out + contract_cols(dv_ref[pair_rows(c), :], wkv_ref[1, block, :])
            near_part[c, :, block] = out.astype(jnp.bfloat16)

        turn = lax.rem(c, share_spans)

        @pl.when(jnp.logical_and(sec == 0, owner > 0))
        def _():
            send(
                near_part.at[c],
                front_recv.at[0, turn],
                near_send.at[c],
                front_sem.at[0, turn],
                {"section": owner},
            )

        @pl.when(jnp.logical_and(sec == 1, even(owner)))
        def _():
            send(
                near_part.at[c],
                front_recv.at[1, turn],
                near_send.at[c],
                front_sem.at[1, turn],
                {"section": owner},
            )

        @pl.when(jnp.logical_and(sec == 0, owner == 0))
        def _():
            front_recv[0, turn] = near_part[c]

        @pl.when(jnp.logical_and(by_plane(owner), c != ten))
        def _():
            send(
                near_part.at[c],
                plane_recv.at[lax.rem(ten - c + n_tensor, n_tensor) - 1],
                near_send.at[c],
                plane_sem,
                {"tensor": c},
            )

    last = sec == n_section - 1

    def each(count, step):
        def body(i, carry):
            step(i)
            return carry

        lax.fori_loop(0, count, body, 0)

    block_cols = 256

    def turn_inputs(j):
        block = pl.ds(pl.multiple_of(j * block_cols, block_cols), block_cols)
        in_turned[block, :] = in_ref[:, block].T
        raw_turned[block, :] = raw_ref[:, block].T
        wkv_ref[0, block, :] = pair_ref[block, 0, :]
        wkv_ref[1, block, :] = pair_ref[block, 1, :]

    def weight_grads(j):
        block = pl.ds(pl.multiple_of(j * block_cols, block_cols), block_cols)
        grad_query = jnp.dot(in_turned[block, :], dq_ref[...], preferred_element_type=jnp.float32)
        query_ref[block, :] = grad_query.astype(jnp.bfloat16)
        grad_key = jnp.dot(raw_turned[block, :], dk_ref[...], preferred_element_type=jnp.float32)
        pair_ref[block, 0, :] = grad_key.astype(jnp.bfloat16)
        grad_value = jnp.dot(raw_turned[block, :], dv_ref[...], preferred_element_type=jnp.float32)
        pair_ref[block, 1, :] = grad_value.astype(jnp.bfloat16)
        grad_outer = contract_rows(att_ref[...], g_ref[:, block])
        outer_ref[:, block] = grad_outer.astype(jnp.bfloat16)

    blocks = width // block_cols

    @pl.when(jnp.logical_not(last))
    def _():
        each(spans, share)
        each(spans, relay)
        for weight in weights:
            weight.wait()
        each(spans, stage_p)
        each(blocks, turn_inputs)

    @pl.when(last)
    def _():
        share(0)

    keep, quarter = near_ref.shape[0], NTOK // near_ref.shape[0]
    home = ten // share_spans
    first_peer = lax.rem(ten, share_spans) * quarter

    def spread(turn):
        @pl.when(sec > 0)
        def _():
            wait_bytes(front_recv.at[0, turn], front_sem.at[0, turn])

        @pl.when(even(sec))
        def _():
            wait_bytes(front_recv.at[1, turn], front_sem.at[1, turn])
            for piece in range(quarter):
                rows = slice(piece * keep, (piece + 1) * keep)
                total = front_recv[0, turn, rows, :].astype(jnp.float32)
                total = total + front_recv[1, turn, rows, :].astype(jnp.float32)
                front_recv[0, turn, rows, :] = total.astype(jnp.bfloat16)

        for step in range(quarter):
            piece = lax.rem(ten + step, quarter)
            peer = turn * quarter + piece

            @pl.when(peer != ten)
            def _():
                send(
                    front_recv.at[0, turn, pl.ds(pl.multiple_of(piece * keep, keep), keep)],
                    sum_recv.at[lax.rem(ten - peer + n_tensor, n_tensor) - 1],
                    sum_send,
                    sum_sem,
                    {"tensor": peer},
                )

    far_spans = spans - share_spans

    def neighbour_terms(j):
        c = jnp.where(j < far_spans, share_spans + lax.rem(ten + j, far_spans), j - far_spans)
        stage_k(c)
        stage_n(c)

    def tick(t, carry):
        first = t < spans
        second = jnp.logical_and(t > 0, t <= spans)

        @pl.when(first)
        def _():
            stage_a(t)

        @pl.when(t > 2)
        def _():
            stage_d(t - 3)

        @pl.when(jnp.logical_and(last, jnp.logical_and(first, t > 0)))
        def _():
            stage_p(t)

        @pl.when(first)
        def _():
            stage_a2(t)

        @pl.when(jnp.logical_and(last, t < 3))
        def _():
            @pl.when(t == 0)
            def _():
                share(1)

            share(2 * t + 2)
            share(2 * t + 3)

        @pl.when(jnp.logical_and(last, t == 0))
        def _():
            relay(0)
            stage_p(0)
            for weight in weights:
                weight.wait()

        @pl.when(jnp.logical_and(last, t < spans - 1))
        def _():
            relay(t + 1)

        @pl.when(jnp.logical_and(sec == 0, jnp.logical_and(t > 1, t < spans + 2)))
        def _():
            stage_k(span_at(t - 2))
            stage_n(span_at(t - 2))

        @pl.when(second)
        def _():
            stage_bc(t - 1)

        return carry

    lax.fori_loop(0, spans + 3, tick, 0)

    outs = [
        pltpu.make_async_copy(query_ref, query_out, copy_sem.at[0]),
        pltpu.make_async_copy(pair_ref, pair_out, copy_sem.at[1]),
        pltpu.make_async_copy(outer_ref, outer_out, copy_sem.at[2]),
        pltpu.make_async_copy(streams_ref, streams_out, copy_sem.at[5]),
    ]

    near_copy = pltpu.make_async_copy(near_ref, near_out, copy_sem.at[6])

    @pl.when(sec > 0)
    def _():
        each(spans, stage_s)

    @pl.when(last)
    def _():
        each(blocks, turn_inputs)

    @pl.when(sec > 0)
    def _():
        each(spans, neighbour_terms)

    @pl.when(sec == 1)
    def _():
        each(share_spans, spread)

    @pl.when(sec > 0)
    def _():
        each(blocks, weight_grads)
        for out in outs[:-1]:
            out.start()

    @pl.when(by_plane(home))
    def _():
        wait_bytes(plane_recv, plane_sem)
        for piece in range(quarter):
            rows = slice(piece * keep, (piece + 1) * keep)
            total = near_part[ten, rows, :].astype(jnp.float32)
            for slot in range(n_tensor - 1):
                total = total + plane_recv[slot, rows, :].astype(jnp.float32)
            plane_sum[piece] = total.astype(jnp.bfloat16)
            here = jnp.logical_and(home == sec, first_peer + piece == ten)

            @pl.when(here)
            def _():
                far_recv[sec - 1] = plane_sum[piece]

            @pl.when(jnp.logical_not(here))
            def _():
                send(
                    plane_sum.at[piece],
                    far_recv.at[sec - 1],
                    far_send.at[piece],
                    far_sem.at[sec - 1],
                    {"section": home, "tensor": first_peer + piece},
                )

    @pl.when(sec != 1)
    def _():
        each(share_spans, spread)

    @pl.when(sec == 0)
    def _():
        each(spans, stage_s)
        each(blocks, weight_grads)
        for out in outs[:-1]:
            out.start()

    @pl.when(even(sec))
    def _():
        far_recv[0] = jnp.zeros(far_recv.shape[1:], far_recv.dtype)

    wait_bytes(part_recv.at[0], stream_sem)
    outs[-1].start()
    source = sec * share_spans + ten // quarter
    for slot in range(n_section - 1):

        comes = jnp.logical_not(jnp.logical_and(sec == slot + 1, source == ten))
        if slot == 0:
            comes = jnp.logical_and(comes, jnp.logical_not(even(sec)))

        @pl.when(comes)
        def _():
            wait_bytes(far_recv.at[slot], far_sem.at[slot])

    wait_bytes(sum_recv, sum_sem)
    own = pl.ds(pl.multiple_of(lax.rem(ten, quarter) * keep, keep), keep)
    total = front_recv[0, ten // quarter, own, :].astype(jnp.float32)
    for slot in range(n_tensor - 1):
        total = total + sum_recv[slot].astype(jnp.float32)
    for slot in range(n_section - 1):
        total = total + far_recv[slot].astype(jnp.float32)
    near_ref[...] = total.astype(jnp.bfloat16)
    near_copy.start()

    def drain(c, carry):
        wait_bytes(pair_recv.at[c], pair_send.at[c])
        wait_bytes(z_recv.at[c], z_send.at[c])
        wait_bytes(part_recv.at[c], part_send.at[c])

        @pl.when(c // owned == dpp)
        def _():
            wait_bytes(qkv.at[pl.ds(0, 2)], qkv_send.at[c])

        @pl.when(c // owned == across)
        def _():
            wait_bytes(qkv.at[c], qkv_send.at[c])

        owner = c // share_spans
        front = jnp.logical_or(
            jnp.logical_and(sec == 0, owner > 0), jnp.logical_and(sec == 1, even(owner))
        )

        @pl.when(jnp.logical_or(front, jnp.logical_and(by_plane(owner), c != ten)))
        def _():
            wait_bytes(near_part.at[c], near_send.at[c])

        @pl.when(sec > 0)
        def _():
            wait_bytes(g_ref.at[token_rows(c)], g_send.at[c])

        @pl.when(c != ten)
        def _():
            wait_bytes(new_ref.at[c], stream_send.at[c])

        return carry

    lax.fori_loop(0, spans, drain, 0)
    wait_bytes(sum_recv, sum_send)
    for piece in range(quarter):

        @pl.when(jnp.logical_and(by_plane(home), jnp.logical_not(jnp.logical_and(home == sec, first_peer + piece == ten))))
        def _():
            wait_bytes(plane_sum.at[piece], far_send.at[piece])

    for out in outs:
        out.wait()
    near_copy.wait()


def run_chain(cotangent, queries, pairs, weight_query, weight_out, weight_pair, streams_in, neighbours):
    n_section = lax.axis_size("section")
    n_tensor = lax.axis_size("tensor")
    n_dp = lax.axis_size("dp")
    total, width = cotangent.shape
    feats = queries.shape[1]
    mrows = neighbours.shape[0]
    heads = feats // HDIM
    spans = total // SPAN
    cols = width // n_tensor
    keep = mrows // (n_section * n_tensor)
    turns = spans // n_section
    bf16, f32 = jnp.bfloat16, jnp.float32
    vmem = pl.BlockSpec(memory_space=pltpu.VMEM)
    anywhere = pl.BlockSpec(memory_space=pl.ANY)
    dma = pltpu.SemaphoreType.DMA
    return pl.pallas_call(
        functools.partial(chain_kernel, n_section, n_tensor, n_dp),
        out_shape=[
            jax.ShapeDtypeStruct((SPAN, width), bf16),
            jax.ShapeDtypeStruct((keep, width), bf16),
            jax.ShapeDtypeStruct((width, feats), bf16),
            jax.ShapeDtypeStruct((width, 2, feats), bf16),
            jax.ShapeDtypeStruct((feats, width), bf16),
        ],
        in_specs=[anywhere, vmem, vmem, anywhere, vmem, anywhere, anywhere, anywhere],
        out_specs=[anywhere] * 5,
        scratch_shapes=[
            pltpu.VMEM((total, width), bf16),
            pltpu.VMEM((spans, SPAN + 2 * NTOK, feats), bf16),
            pltpu.VMEM((spans, SPAN, feats), bf16),
            pltpu.VMEM((spans, SPAN, feats), bf16),
            pltpu.VMEM((spans, SPAN, feats), bf16),
            pltpu.VMEM((spans, SPAN, feats), bf16),
            pltpu.VMEM((spans, n_tensor - 1, SPAN, cols), bf16),
            pltpu.VMEM((spans, SPAN, cols), f32),
            pltpu.VMEM((spans, n_tensor - 1, SPAN, cols), bf16),
            pltpu.VMEM((spans, SPAN, cols), bf16),
            pltpu.VMEM((SPAN, width), bf16),
            pltpu.VMEM((total, feats), bf16),
            pltpu.VMEM((total, feats), bf16),
            pltpu.VMEM((mrows, feats), bf16),
            pltpu.VMEM((mrows, feats), bf16),
            pltpu.VMEM((spans, heads, SPAN, NTOK), f32),
            pltpu.VMEM((spans, heads, SPAN, NTOK), bf16),
            pltpu.VMEM((spans, SPAN, feats), bf16),
            pltpu.VMEM((spans, heads, SPAN, NTOK), bf16),
            pltpu.VMEM((width, feats), bf16),
            pltpu.VMEM((2, width, feats), bf16),
            pltpu.VMEM((total, width), bf16),
            pltpu.VMEM((mrows, width), bf16),
            pltpu.VMEM((width, total), bf16),
            pltpu.VMEM((width, mrows), bf16),
            pltpu.VMEM((width, feats), bf16),
            pltpu.VMEM((width, 2, feats), bf16),
            pltpu.VMEM((feats, width), bf16),
            pltpu.VMEM((spans, NTOK, width), bf16),
            pltpu.VMEM((2, turns, NTOK, width), bf16),
            pltpu.VMEM((n_tensor - 1, NTOK, width), bf16),
            pltpu.VMEM((NTOK // keep, keep, width), bf16),
            pltpu.VMEM((n_section - 1, keep, width), bf16),
            pltpu.VMEM((n_tensor - 1, keep, width), bf16),
            pltpu.VMEM((keep, width), bf16),
            dma((7,)),
            dma((spans,)),
            dma((spans,)),
            dma((spans,)),
            dma((spans,)),
            dma((spans,)),
            dma((spans,)),
            dma((spans,)),
            dma((spans,)),
            dma((spans,)),
            dma((spans,)),
            dma((spans,)),
            dma,
            dma((spans,)),
            dma((2, turns)),
            dma,
            dma((NTOK // keep,)),
            dma((n_section - 1,)),
            dma,
            dma,
        ],
        compiler_params=pltpu.CompilerParams(
            collective_id=0, has_side_effects=True, vmem_limit_bytes=60 * 2**20
        ),
    )(cotangent, queries, pairs, weight_query, weight_out, weight_pair, streams_in, neighbours)


def on_device(cotangent, queries, keys_values, streams_in, neighbours, w_query, w_key_value, w_out):
    results = run_chain(
        cotangent,
        queries[0],
        jnp.swapaxes(keys_values[0], 0, 1),
        w_query[0],
        w_out[0],
        w_key_value[0],
        streams_in[0],
        neighbours,
    )
    streams, neighbour_part, grad_query, grad_pair, grad_out = results
    return (streams[None], neighbour_part, grad_query[None], grad_pair[None], grad_out[None])


def solution(mesh):
    in_specs = (
        P(None, "dp"),
        P("section", "dp", "tensor"),
        P("section", "dp", None, "tensor"),
        P("section", None, "dp"),
        P(None, "dp"),
        P("section", "dp", "tensor"),
        P("section", "dp", None, "tensor"),
        P("section", "tensor", "dp"),
    )
    out_specs = (
        P("section", "tensor", "dp"),
        P(("section", "tensor"), "dp"),
        P("section", "dp", "tensor"),
        P("section", "dp", None, "tensor"),
        P("section", "tensor", "dp"),
    )
    return jax.shard_map(
        on_device, mesh=mesh, in_specs=in_specs, out_specs=out_specs, check_vma=False
    )
```
